256 devices in a mesh: ctx: 32 (over x, z), mp: 8 (over y, core).
Axes of the slice: x: 4, y: 4, z: 8, core: 2. Of those that a mesh axis runs over, the one named last changes fastest.
Arguments:
- gate_rows: bfloat16 [4096, 8192], P(('ctx', 'mp')), may hold values from -6 to 6
- key_rows: bfloat16 [4096, 8192], P(('ctx', 'mp')), may hold values from -6 to 6
- value_rows: bfloat16 [4096, 8192], P(('ctx', 'mp')), may hold values from -6 to 6
- out_grad: bfloat16 [4096, 8192], P(('ctx', 'mp')), may hold values from -12 to 12
- conv_taps: float32 [3, 3, 8192], P(None, None, 'mp'), may hold values from -3 to 3
- filter_residues: float32 [512, 16], P('mp'), may hold values from -3 to 3
- filter_poles: float32 [512, 16], P('mp'), may hold values from 0.96 to 1, as said below
- skip_gain: float32 [8192], P('mp'), may hold values from -3 to 3
- seq_lengths: int32 [8], replicated, may hold values from 1 to 2048, 4096 in all
- piece_list: int32 [32], replicated, may hold values from 0 to 31, each once
Outputs:
- mixed_out: bfloat16 [4096, 8192], P(('ctx', 'mp'))
- gate_grad: bfloat16 [4096, 8192], P(('ctx', 'mp'))
- key_grad: bfloat16 [4096, 8192], P(('ctx', 'mp'))
- value_grad: bfloat16 [4096, 8192], P(('ctx', 'mp'))
- taps_grad: float32 [3, 3, 8192], P(None, None, 'mp')
- skip_grad: float32 [8192], P('mp')
The draws below stay inside these ranges and needn't reach their ends.
Inputs may be any that keep to these rules, and one draw needn't show every extreme that they name: `seq_lengths`: the genomes' lengths sum to 4096; the longest is exactly 2048. `piece_list`: each piece number appears once. `filter_poles`: poles are below 1.
All inputs are finite; a program needn't handle non-finite values.
Results may differ from the reference program's by a relative error of at most 0.00245.
Values may be sent and summed in bfloat16 or wider, within the bound.
No kernel may reach another device: no remote copies, remote signals or barrier semaphores. Data moves between devices by JAX's collectives and lax.ppermute only.
A program may use at most 128 MiB of HBM per device.

```python
import math
import jax
import jax.numpy as jnp
import numpy as np
from jax import lax

D = 8192
GROUP = 16
MODES = 16
PIECE = 128
NSEQ = 8
NPIECES = 32
TOKENS = 4096
GROUPS = 512


def draw_out_grad(key, part):
    key = jax.random.fold_in(key, 11)
    position = jnp.arange(TOKENS, dtype=jnp.float32)[:, None] / TOKENS
    base = jnp.clip(jax.random.normal(key, (TOKENS, D), jnp.float32), -4.0, 4.0)
    ramp = 1.0 + 2.0 * position
    return (base * ramp).astype(jnp.bfloat16)


def draw_filter_poles(key, part):
    key = jax.random.fold_in(key, 23)
    pick_key, slow_key, fast_key = jax.random.split(key, 3)
    share = 0.5
    slow_pick = jax.random.bernoulli(pick_key, share, (GROUPS, MODES))
    slow_rate = jnp.exp(jax.random.uniform(slow_key, (GROUPS, MODES), jnp.float32, jnp.log(0.25 / TOKENS), jnp.log(2.0 / TOKENS)))
    fast_rate = jnp.exp(jax.random.uniform(fast_key, (GROUPS, MODES), jnp.float32, jnp.log(2.0 / TOKENS), jnp.log(1.0 / 30.0)))
    rate = jnp.where(slow_pick, slow_rate, fast_rate)
    return jnp.exp(-rate).astype(jnp.float32)


def block_scale(own_key, shape, cuts, low, high):
    loudness, own = 1.0, jax.random.fold_in(own_key, 6)
    for dim, parts in cuts:
        steps = jnp.exp(jax.random.uniform(jax.random.fold_in(own, dim), (parts,), jnp.float32, low / len(cuts), high / len(cuts)))
        loudness = loudness * jnp.repeat(steps, shape[dim] // parts).reshape([-1 if axis == dim else 1 for axis in range(len(shape))])
    return loudness


def length_profile(number_of, total, most, lean):
    portions = [(1 << 20) // math.isqrt(grade ** lean) + 1 for grade in range(2, number_of + 1)]
    surplus, given = total - most - (number_of - 1), [1] * (number_of - 1)
    while surplus > 0:
        free = [i for i in range(number_of - 1) if given[i] < most]
        mass, remaining = sum([portions[i] for i in free]), surplus
        for i in free:
            extra = min(most - given[i], max(1, remaining * portions[i] // mass), surplus)
            given[i] = given[i] + extra
            surplus = surplus - extra
    return np.array([most] + given)


def ragged(rng, number_of, total, most, lean):
    if number_of == 2:
        one = jax.random.randint(rng, (), max(1, total - most), min(most, total - 1) + 1)
        return jnp.stack([one, total - one])
    sizes = jnp.asarray(length_profile(number_of, total, most, lean), jnp.int32)
    couples = (number_of - 1) // 2
    giver, taker = sizes[1:1 + 2 * couples:2], sizes[2:2 + 2 * couples:2]
    slack = jnp.minimum(giver - 1, most - taker)
    passed = jax.random.randint(jax.random.fold_in(rng, 1), (couples,), 0, 1 << 20) % (slack + 1)
    sizes = sizes.at[1:1 + 2 * couples:2].set(giver - passed).at[2:2 + 2 * couples:2].set(taker + passed)
    return sizes[jax.random.permutation(jax.random.fold_in(rng, 2), number_of)]


def bell_draw(own_key, shape, spread, reach, shards=(), held_as=jnp.bfloat16):
    result = jax.random.normal(own_key, shape, jnp.float32) * spread
    if len(shards) > 0:
        result = block_scale(own_key, shape, shards, -0.22, 0.18) * result
    return jnp.clip(result, min=-reach, max=reach).astype(held_as)


def setup_inputs(seed: int = 0) -> dict:
    keys = jax.random.split(jax.random.key(seed), 11)
    return {
        "gate_rows": bell_draw(keys[0], (TOKENS, D), 1.0, 6.0, ((0, 256),)),
        "key_rows": bell_draw(keys[1], (TOKENS, D), 1.0, 6.0, ((0, 256),)),
        "value_rows": bell_draw(keys[2], (TOKENS, D), 1.0, 6.0, ((0, 256),)),
        "out_grad": draw_out_grad(jax.random.fold_in(keys[10], 71), 0),
        "conv_taps": bell_draw(keys[4], (3, 3, D), 0.6, 3.0, ((2, 8),), jnp.float32),
        "filter_residues": bell_draw(keys[5], (GROUPS, MODES), 0.5, 3.0, ((0, 8),), jnp.float32),
        "filter_poles": draw_filter_poles(jax.random.fold_in(keys[10], 71), 0),
        "skip_gain": bell_draw(keys[7], (D,), 0.5, 3.0, ((0, 8),), jnp.float32),
        "seq_lengths": ragged(keys[8], NSEQ, TOKENS, TOKENS // 2, 2).astype(jnp.int32),
        "piece_list": jax.random.permutation(keys[9], NPIECES).astype(jnp.int32),
    }


def delayed(values, delay, valid):
    if delay == 0:
        return values
    padded = jnp.concatenate([jnp.zeros((delay, values.shape[1]), values.dtype), values[:-delay]], axis=0)
    return padded * valid[:, None]

def advanced(values, delay, valid):
    if delay == 0:
        return values
    masked = values * valid[:, None]
    return jnp.concatenate([masked[delay:], jnp.zeros((delay, values.shape[1]), values.dtype)], axis=0)

def reference(gate_rows, key_rows, value_rows, out_grad, conv_taps, filter_residues, filter_poles, skip_gain, seq_lengths, piece_list):
    slots = jnp.arange(NPIECES, dtype=jnp.int32)
    inverse = jnp.zeros((NPIECES,), jnp.int32).at[piece_list].set(slots)
    row_ids = jnp.arange(TOKENS, dtype=jnp.int32)
    bounds = jnp.cumsum(seq_lengths).astype(jnp.int32)
    segment = lax.optimization_barrier(jnp.sum((bounds[None, :] <= row_ids[:, None]).astype(jnp.int32), axis=1))
    link_one = jnp.concatenate([jnp.zeros((1,), jnp.float32), (segment[1:] == segment[:-1]).astype(jnp.float32)])
    link_two = jnp.concatenate([jnp.zeros((2,), jnp.float32), (segment[2:] == segment[:-2]).astype(jnp.float32)])
    links = (None, link_one, link_two)
    fresh = 1.0 - link_one
    width = math.gcd(D, 1024)
    blocks = D // width

    def to_blocks(values):
        ordered = values.reshape(NPIECES, PIECE, D)[inverse].reshape(TOKENS, D)
        return ordered.reshape(TOKENS, blocks, width).transpose(1, 0, 2)

    def from_blocks(values):
        ordered = values.transpose(1, 0, 2).reshape(TOKENS, D)
        return ordered.reshape(NPIECES, PIECE, D)[piece_list].reshape(TOKENS, D)
    mode_scale = filter_residues * jnp.sqrt(1.0 - filter_poles * filter_poles)
    decays = jnp.repeat(filter_poles, GROUP, axis=0).T.reshape(MODES, blocks, width).transpose(1, 0, 2)
    scales = jnp.repeat(mode_scale, GROUP, axis=0).T.reshape(MODES, blocks, width).transpose(1, 0, 2)
    taps = conv_taps.reshape(3, 3, blocks, width).transpose(2, 0, 1, 3)
    gains = skip_gain.reshape(blocks, width)
    norm = 1.0 / math.sqrt(TOKENS)

    def work(pieces):
        gate, keyed_in, value, grad_out, tap_rows, decay_rate, weight, gain = pieces
        inputs = [gate.astype(jnp.float32), keyed_in.astype(jnp.float32), value.astype(jnp.float32)]
        empty = jnp.zeros((TOKENS, width), jnp.float32)
        feats = []
        for member in range(3):
            total = empty
            for delay in range(3):
                total = total + tap_rows[member, delay][None, :] * delayed(inputs[member], delay, links[delay])
            feats.append(total)
        front, keyed, valued = feats
        mixed = keyed * valued

        def forward_step(state, inputs_row):
            row_value, start = inputs_row
            state = decay_rate * state * (1.0 - start) + row_value[None, :]
            return (state, lax.optimization_barrier(jnp.sum(weight * state, axis=0)))
        _, modal = lax.scan(forward_step, jnp.zeros((MODES, width), jnp.float32), (mixed, fresh))
        filtered = modal + gain[None, :] * mixed
        output = (front * filtered).astype(jnp.bfloat16)
        upstream = grad_out.astype(jnp.float32)
        grad_filtered = upstream * front
        grad_front = upstream * filtered

        def backward_step(state, inputs_row):
            row_value, start = inputs_row
            current = row_value[None, :] + decay_rate * state
            return (current * (1.0 - start), lax.optimization_barrier(jnp.sum(weight * current, axis=0)))
        _, back_modal = lax.scan(backward_step, jnp.zeros((MODES, width), jnp.float32), (grad_filtered, fresh), reverse=True)
        grad_mixed = back_modal + gain[None, :] * grad_filtered
        grads = [grad_front, grad_mixed * valued, grad_mixed * keyed]
        input_grads = []
        tap_terms = []
        for member in range(3):
            total = empty
            row_terms = []
            for delay in range(3):
                total = total + tap_rows[member, delay][None, :] * advanced(grads[member], delay, links[delay])
                row_terms.append(lax.optimization_barrier(jnp.sum(grads[member] * delayed(inputs[member], delay, links[delay]), axis=0)))
            input_grads.append(total.astype(jnp.bfloat16))
            tap_terms.append(jnp.stack(row_terms))
        tap_grad = jnp.stack(tap_terms) * norm
        skip_part = lax.optimization_barrier(jnp.sum(grad_filtered * mixed, axis=0)) * norm
        return (output, input_grads[0], input_grads[1], input_grads[2], tap_grad, skip_part)
    results = lax.map(work, (to_blocks(gate_rows), to_blocks(key_rows), to_blocks(value_rows), to_blocks(out_grad), taps, decays, scales, gains))
    mixed_out = from_blocks(results[0])
    gate_grad = from_blocks(results[1])
    key_grad = from_blocks(results[2])
    value_grad = from_blocks(results[3])
    taps_grad = results[4].transpose(1, 2, 0, 3).reshape(3, 3, D)
    skip_grad = results[5].reshape(D)
    return (mixed_out, gate_grad, key_grad, value_grad, taps_grad, skip_grad)
```

```python
import math

import jax
import jax.numpy as jnp
from jax import lax
from jax.experimental import pallas as pl
from jax.experimental.pallas import tpu as pltpu
from jax.sharding import PartitionSpec as P

BOTH = ("ctx", "mp")
PIECE = 128
NPIECES = 32
NSEQ = 8
MODES = 16
OWN = 32
TOKENS = 4096
BASE = NPIECES * 16
VROWS = BASE + NSEQ * 16
F32 = jnp.float32
BF16 = jnp.bfloat16


def lane_ids(shape):
    return lax.broadcasted_iota(jnp.int32, shape, 1)


def swap_blocks(tiles):
    lane = lane_ids(tiles[0].shape)
    low = lane < 64
    even = (lane & 32) == 0
    a, b, c, d = tiles
    n0 = jnp.where(low, a, pltpu.roll(c, 64, 1))
    n2 = jnp.where(low, pltpu.roll(a, 64, 1), c)
    n1 = jnp.where(low, b, pltpu.roll(d, 64, 1))
    n3 = jnp.where(low, pltpu.roll(b, 64, 1), d)
    m0 = jnp.where(even, n0, pltpu.roll(n1, 32, 1))
    m1 = jnp.where(even, pltpu.roll(n0, 96, 1), n1)
    m2 = jnp.where(even, n2, pltpu.roll(n3, 32, 1))
    m3 = jnp.where(even, pltpu.roll(n2, 96, 1), n3)
    return m0, m1, m2, m3


def pack_kernel(a_ref, b_ref, c_ref, d_ref, o_ref):
    for j in range(8):
        for q in range(8):
            cols = slice(j * 1024 + q * 128, j * 1024 + (q + 1) * 128)
            tiles = [ref[:, cols].astype(F32) for ref in (a_ref, b_ref, c_ref, d_ref)]
            for k, tile in enumerate(swap_blocks(tiles)):
                o_ref[(4 * q + k) * 8 + j] = tile.astype(BF16)


def unpack_kernel(x_ref, a_ref, b_ref, c_ref, d_ref):
    for j in range(8):
        for q in range(8):
            cols = slice(j * 1024 + q * 128, j * 1024 + (q + 1) * 128)
            tiles = [x_ref[(4 * q + k) * 8 + j].astype(F32) for k in range(4)]
            for ref, tile in zip((a_ref, b_ref, c_ref, d_ref), swap_blocks(tiles)):
                ref[:, cols] = tile.astype(BF16)


def split(values):
    high = values.astype(BF16)
    return high, (values - high.astype(F32)).astype(BF16)


def dot3(left, right):
    def dot(a, b):
        return jnp.dot(a, b, preferred_element_type=F32)

    return dot(left[0], right[0]) + (dot(left[1], right[0]) + dot(left[0], right[1]))


(M_ONE, M_TWO, L_ONE, L_TWO, FIRST, TAIL, NOTBEG, NEXTCONT, WHOLE) = range(9)


def main_kernel(
    lens_ref, list_ref, here_ref, x_ref, taps_ref, res_ref, pole_ref, gain_ref,
    y_ref, g_ref,
    inv_ref, mask_ref, prep_ref, tapb_ref, gainb_ref,
    tf_ref, tb_ref, we_ref, wh_ref, wr_ref, ws_ref,
    xt_ref, feat_ref, z_ref, gu_ref,
    lzf_ref, lzt_ref, lgt_ref, lgf_ref,
    u_ref, gz_ref, e_ref, h_ref, roll_ref, acc_ref,
):
    here = here_ref[0]
    begins = [jnp.int32(0)]
    for k in range(NSEQ):
        begins.append(begins[-1] + lens_ref[k])

    def invert(s, carry):
        inv_ref[list_ref[s]] = s
        return carry

    lax.fori_loop(0, NPIECES, invert, 0)

    shape = (NPIECES, PIECE)
    base = lax.broadcasted_iota(jnp.int32, shape, 0) * PIECE
    row = base + lane_ids(shape)

    def count(ids, upto=NSEQ):
        total = jnp.zeros(shape, jnp.int32)
        for k in range(upto):
            total = total + (begins[k] <= ids).astype(jnp.int32)
        return total

    def starts(ids):
        hit = ids == begins[0]
        for k in range(1, NSEQ + 1):
            hit = hit | (ids == begins[k])
        return hit

    own = count(row)
    at_first, at_last, before = count(base), count(base + PIECE - 1), count(base - 1)
    here_start, prior_start = starts(row), starts(row - 1)
    next_start, after_start = starts(row + 1), starts(row + 2)
    one = jnp.ones(shape, F32)
    zero = jnp.zeros(shape, F32)
    mask_ref[M_ONE] = jnp.where(here_start, zero, one)
    mask_ref[M_TWO] = jnp.where(here_start | prior_start, zero, one)
    mask_ref[L_ONE] = jnp.where(next_start, zero, one)
    mask_ref[L_TWO] = jnp.where(next_start | after_start, zero, one)
    mask_ref[FIRST] = jnp.where(own == at_first, one, zero)
    mask_ref[TAIL] = jnp.where(own == at_last, one, zero)
    mask_ref[NOTBEG] = jnp.where(at_first == before, one, zero)
    mask_ref[NEXTCONT] = jnp.where(starts(base + PIECE), zero, one)
    mask_ref[WHOLE] = jnp.where(at_first == at_last, one, zero)

    block = pl.ds(pl.multiple_of((here // 4) * 128, 128), 128)
    shift = lax.rem(128 - 32 * lax.rem(here, 4), 128)
    prep_ref[...] = jnp.zeros((PIECE, PIECE), F32)
    for a in range(3):
        for j in range(3):
            prep_ref[a * 3 + j : a * 3 + j + 1, :] = taps_ref[a, j : j + 1, block]
    prep_ref[9:10, :] = gain_ref[0:1, block]
    prep_ref[0:16, :] = pltpu.roll(prep_ref[0:16, :], shift, 1)
    prep_ref[16:18, 0:MODES] = pole_ref[pl.ds(2 * here, 2), :]
    prep_ref[24:26, 0:MODES] = res_ref[pl.ds(2 * here, 2), :]
    turned = prep_ref[...].T

    def column(rows, at):
        return jnp.broadcast_to(turned[0:rows, at : at + 1], (rows, PIECE))

    for j in range(3):
        for a in range(3):
            tapb_ref[j, a * OWN : (a + 1) * OWN, :] = column(OWN, a * 3 + j)
    gainb_ref[...] = column(OWN, 9)
    pole = jnp.concatenate([column(MODES, 16), column(MODES, 17)], axis=0)
    residue = jnp.concatenate([column(MODES, 24), column(MODES, 25)], axis=0)
    weight = residue * jnp.sqrt(1.0 - pole * pole)
    lane = lane_ids((2 * MODES, PIECE))
    powers = jnp.ones((2 * MODES, PIECE), F32)
    falling = powers
    square = pole
    for bit in range(7):
        up = ((lane >> bit) & 1) == 1
        powers = jnp.where(up, powers * square, powers)
        falling = jnp.where(up, falling, falling * square)
        square = square * square
    rising = weight * (powers * pole)
    shrinking = weight * (falling * pole)
    taper = weight * powers

    sub_ids = lax.broadcasted_iota(jnp.int32, (PIECE, PIECE), 0)
    col_ids = lane_ids((PIECE, PIECE))
    tf_ref[...] = jnp.zeros(tf_ref.shape, BF16)
    tb_ref[...] = jnp.zeros(tb_ref.shape, BF16)
    wr_ref[...] = jnp.zeros(wr_ref.shape, BF16)
    ws_ref[...] = jnp.zeros(ws_ref.shape, BF16)
    for g in range(2):
        line = jnp.sum(taper[g * MODES : (g + 1) * MODES], axis=0, keepdims=True)
        spread = pltpu.roll(
            jnp.broadcast_to(line, (PIECE, PIECE)), 0, 1, stride=1, stride_axis=0
        )
        toeplitz = jnp.where(col_ids >= sub_ids, spread, 0.0)
        at = slice(g * PIECE, (g + 1) * PIECE)
        for part, tile in enumerate(split(toeplitz)):
            tf_ref[part, at, at] = tile
        for part, tile in enumerate(split(toeplitz.T)):
            tb_ref[part, at, at] = tile
        for ref, source in ((wr_ref, rising), (ws_ref, shrinking)):
            high, low = split(source[g * MODES : (g + 1) * MODES])
            ref[g * MODES : (g + 1) * MODES, at] = high
            ref[32 + g * MODES : 32 + (g + 1) * MODES, at] = high
            ref[64 + g * MODES : 64 + (g + 1) * MODES, at] = low
    blank = jnp.zeros((32, PIECE), F32)
    fall_cols = jnp.concatenate([falling, falling, falling, blank], axis=0).T
    power_cols = jnp.concatenate([powers, powers, powers, blank], axis=0).T
    group_zero = (col_ids & 16) == 0
    for ref, cols in ((we_ref, fall_cols), (wh_ref, power_cols)):
        for part, tile in enumerate(split(cols)):
            wide = tile.astype(F32)
            ref[part, 0:PIECE, :] = jnp.where(group_zero, wide, 0.0).astype(BF16)
            ref[part, PIECE:, :] = jnp.where(group_zero, 0.0, wide).astype(BF16)
    leap = fall_cols[0:1, :] * fall_cols[126:127, :]

    def store_lhs(ref, at, values):
        for part, tile in enumerate(split(values)):
            ref[part, pl.ds(at, 16), 0:PIECE] = tile[0:16]
            ref[part, pl.ds(at, 16), PIECE:] = tile[16:32]

    edge = lane_ids((96, PIECE))
    roll_ref[...] = jnp.zeros(roll_ref.shape, F32)
    acc_ref[...] = jnp.zeros(acc_ref.shape, F32)

    def ahead(p, carry):
        slot = inv_ref[p]
        tile = x_ref[pl.ds(slot * 8, 8)].reshape(PIECE, PIECE).astype(F32).T
        xt_ref[p] = tile
        x = tile[0:96]
        back_one = pltpu.roll(x, 1, 1)
        back_two = pltpu.roll(x, 2, 1)
        x_one = jnp.where(edge < 1, roll_ref[0], back_one)
        x_two = jnp.where(edge < 2, roll_ref[1], back_two)
        roll_ref[0] = back_one
        roll_ref[1] = back_two
        feats = (
            tapb_ref[0] * x
            + mask_ref[M_ONE, pl.ds(p, 1), :] * (tapb_ref[1] * x_one)
            + mask_ref[M_TWO, pl.ds(p, 1), :] * (tapb_ref[2] * x_two)
        )
        feat_ref[p] = feats
        z = feats[32:64] * feats[64:96]
        gu = tile[96:128] * feats[0:32]
        z_ref[p] = z
        gu_ref[p] = gu
        acc_ref[0, 96:128, :] += gu * z
        first = mask_ref[FIRST, pl.ds(p, 1), :]
        tail = mask_ref[TAIL, pl.ds(p, 1), :]
        at = pl.multiple_of(p * 16, 16)
        store_lhs(lzf_ref, at, z * first)
        store_lhs(lzt_ref, at, z * tail)
        store_lhs(lgt_ref, at, gu * tail)
        store_lhs(lgf_ref, at, gu * first)
        return carry

    lax.fori_loop(0, NPIECES, ahead, 0, unroll=2)

    line = lane_ids((1, PIECE))
    extras = []
    for k in range(1, NSEQ):
        p = begins[k] // PIECE
        rows = p * PIECE + line
        inner = lax.rem(begins[k], PIECE) != 0
        later = (rows >= begins[k]) & (rows < begins[k + 1]) & inner
        sooner = (rows >= begins[k - 1]) & (rows < begins[k]) & inner
        later = jnp.where(later, 1.0, 0.0)
        sooner = jnp.where(sooner, 1.0, 0.0)
        extras.append((p, later, sooner))
        store_lhs(lzf_ref, BASE + (k - 1) * 16, z_ref[p] * later)
        store_lhs(lgt_ref, BASE + (k - 1) * 16, gu_ref[p] * sooner)
    none = jnp.zeros((OWN, PIECE), F32)
    store_lhs(lzf_ref, VROWS - 16, none)
    store_lhs(lgt_ref, VROWS - 16, none)

    def both(ref):
        return ref[0], ref[1]

    e_ref[...] = dot3(both(lzt_ref), both(we_ref))
    h_ref[...] = dot3(both(lgf_ref), both(wh_ref))

    def scan(step, carry):
        state, back = carry
        p = step
        at = pl.ds(pl.multiple_of(p * 16, 16), 16)
        found = e_ref[at, :]
        state = state * mask_ref[NOTBEG, pl.ds(p, 1), :]
        e_ref[at, :] = state
        state = found + (mask_ref[WHOLE, pl.ds(p, 1), :] * leap) * state
        p = NPIECES - 1 - step
        at = pl.ds(pl.multiple_of(p * 16, 16), 16)
        found = h_ref[at, :]
        back = back * mask_ref[NEXTCONT, pl.ds(p, 1), :]
        h_ref[at, :] = back
        back = found + (mask_ref[WHOLE, pl.ds(p, 1), :] * leap) * back
        return state, back

    idle = jnp.zeros((16, PIECE), F32)
    lax.fori_loop(0, NPIECES, scan, (idle, idle), unroll=4)

    def three(states):
        high = states.astype(BF16).astype(F32)
        lane = lane_ids(states.shape)
        low = (lane >= 32) & (lane < 64)
        return jnp.where(low, states - high, high).astype(BF16)

    u_ref[...] = dot3(both(lzf_ref), both(tf_ref))
    gz_ref[...] = dot3(both(lgt_ref), both(tb_ref))
    u_ref[0:BASE, :] += jnp.dot(three(e_ref[...]), wr_ref[...], preferred_element_type=F32)
    gz_ref[0:BASE, :] += jnp.dot(three(h_ref[...]), ws_ref[...], preferred_element_type=F32)
    for k, (p, later, sooner) in enumerate(extras):
        at = pl.ds(pl.multiple_of(p * 16, 16), 16)
        more = slice(BASE + k * 16, BASE + (k + 1) * 16)
        for ref, mask in ((u_ref, later), (gz_ref, sooner)):
            for half in (slice(0, PIECE), slice(PIECE, 2 * PIECE)):
                ref[at, half] = jnp.where(mask > 0.0, ref[more, half], ref[at, half])

    roll_ref[...] = jnp.zeros(roll_ref.shape, F32)

    def behind(step, carry):
        p = NPIECES - 1 - step
        slot = inv_ref[p]
        at = pl.ds(pl.multiple_of(p * 16, 16), 16)
        u = jnp.concatenate([u_ref[at, 0:PIECE], u_ref[at, PIECE:]], axis=0)
        gz = jnp.concatenate([gz_ref[at, 0:PIECE], gz_ref[at, PIECE:]], axis=0)
        gain = gainb_ref[...]
        filtered = u + gain * z_ref[p]
        out = feat_ref[p, 0:32, :] * filtered
        grad_front = xt_ref[p, 96:128, :] * filtered
        gz = gz + gain * gu_ref[p]
        grads = jnp.concatenate(
            [grad_front, gz * feat_ref[p, 64:96, :], gz * feat_ref[p, 32:64, :]], axis=0
        )
        next_one = pltpu.roll(grads, PIECE - 1, 1)
        next_two = pltpu.roll(grads, PIECE - 2, 1)
        g_one = mask_ref[L_ONE, pl.ds(p, 1), :] * jnp.where(
            edge >= PIECE - 1, roll_ref[0], next_one
        )
        g_two = mask_ref[L_TWO, pl.ds(p, 1), :] * jnp.where(
            edge >= PIECE - 2, roll_ref[1], next_two
        )
        roll_ref[0] = next_one
        roll_ref[1] = next_two
        back = tapb_ref[0] * grads + tapb_ref[1] * g_one + tapb_ref[2] * g_two
        x = xt_ref[p, 0:96, :]
        acc_ref[0, 0:96, :] += grads * x
        acc_ref[1, 0:96, :] += g_one * x
        acc_ref[2, 0:96, :] += g_two * x
        tile = jnp.concatenate([out, back], axis=0).T.astype(BF16)
        y_ref[pl.ds(slot * 8, 8)] = tile.reshape(8, 16, PIECE)
        return carry

    lax.fori_loop(0, NPIECES, behind, 0, unroll=2)
    norm = 1.0 / math.sqrt(TOKENS)
    g_ref[...] = jnp.zeros(g_ref.shape, F32)
    for j in range(3):
        g_ref[j : j + 1, :] = norm * jnp.sum(acc_ref[j].T, axis=0, keepdims=True)


def vmem_params():
    return pltpu.CompilerParams(vmem_limit_bytes=48 * 1024 * 1024)


VM = pl.BlockSpec(memory_space=pltpu.VMEM)
SM = pl.BlockSpec(memory_space=pltpu.SMEM)


def run_pack(*arrays):
    return pl.pallas_call(
        pack_kernel,
        out_shape=jax.ShapeDtypeStruct((256, 16, 128), BF16),
        in_specs=[VM] * 4,
        out_specs=VM,
        compiler_params=vmem_params(),
        name="pack",
    )(*arrays)


def run_unpack(blocks):
    return pl.pallas_call(
        unpack_kernel,
        out_shape=[jax.ShapeDtypeStruct((16, 8192), BF16)] * 4,
        in_specs=[VM],
        out_specs=[VM] * 4,
        compiler_params=vmem_params(),
        name="unpack",
    )(blocks)


def run_main(lens, pieces, here, blocks, taps, residues, poles, gain):
    scratch = [
        pltpu.SMEM((NPIECES,), jnp.int32),
        pltpu.VMEM((9, NPIECES, PIECE), F32),
        pltpu.VMEM((PIECE, PIECE), F32),
        pltpu.VMEM((3, 96, PIECE), F32),
        pltpu.VMEM((OWN, PIECE), F32),
        pltpu.VMEM((2, 256, 256), BF16),
        pltpu.VMEM((2, 256, 256), BF16),
        pltpu.VMEM((2, 256, PIECE), BF16),
        pltpu.VMEM((2, 256, PIECE), BF16),
        pltpu.VMEM((PIECE, 256), BF16),
        pltpu.VMEM((PIECE, 256), BF16),
        pltpu.VMEM((NPIECES, PIECE, PIECE), F32),
        pltpu.VMEM((NPIECES, 96, PIECE), F32),
        pltpu.VMEM((NPIECES, OWN, PIECE), F32),
        pltpu.VMEM((NPIECES, OWN, PIECE), F32),
        pltpu.VMEM((2, VROWS, 256), BF16),
        pltpu.VMEM((2, BASE, 256), BF16),
        pltpu.VMEM((2, VROWS, 256), BF16),
        pltpu.VMEM((2, BASE, 256), BF16),
        pltpu.VMEM((VROWS, 256), F32),
        pltpu.VMEM((VROWS, 256), F32),
        pltpu.VMEM((BASE, PIECE), F32),
        pltpu.VMEM((BASE, PIECE), F32),
        pltpu.VMEM((2, 96, PIECE), F32),
        pltpu.VMEM((3, PIECE, PIECE), F32),
    ]
    return pl.pallas_call(
        main_kernel,
        out_shape=[
            jax.ShapeDtypeStruct((256, 16, 128), BF16),
            jax.ShapeDtypeStruct((8, 128), F32),
        ],
        in_specs=[SM, SM, SM, VM, VM, VM, VM, VM],
        out_specs=[VM, VM],
        scratch_shapes=scratch,
        compiler_params=vmem_params(),
        name="block",
    )(lens, pieces, here, blocks, taps, residues, poles, gain)


def exchange(blocks):
    return lax.all_to_all(blocks, BOTH, split_axis=0, concat_axis=0, tiled=True)


def local(
    gate_rows,
    key_rows,
    value_rows,
    out_grad,
    conv_taps,
    filter_residues,
    filter_poles,
    skip_gain,
    seq_lengths,
    piece_list,
):
    here = lax.axis_index("ctx").astype(jnp.int32).reshape(1)
    blocks = exchange(run_pack(gate_rows, key_rows, value_rows, out_grad))
    results, sums = run_main(
        seq_lengths,
        piece_list,
        here,
        blocks,
        conv_taps,
        filter_residues,
        filter_poles,
        skip_gain.reshape(1, -1),
    )
    every = lax.all_gather(sums, "ctx", axis=0, tiled=False)
    out_rows, gate_back, key_back, value_back = run_unpack(exchange(results))
    tap_total = every[:, 0:3, 0:96].reshape(32, 3, 3, OWN).transpose(2, 1, 0, 3)
    skip_total = every[:, 0, 96:128].reshape(1024)
    return (
        out_rows,
        gate_back,
        key_back,
        value_back,
        tap_total.reshape(3, 3, 1024),
        skip_total,
    )


def solution(mesh):
    rows = P(BOTH, None)
    return jax.shard_map(
        local,
        mesh=mesh,
        in_specs=(
            rows, rows, rows, rows,
            P(None, None, "mp"), P("mp", None), P("mp", None), P("mp"), P(), P(),
        ),
        out_specs=(rows, rows, rows, rows, P(None, None, "mp"), P("mp")),
        check_vma=False,
    )
```

```python
import math

import jax
import jax.numpy as jnp
from jax import lax
from jax.experimental import pallas as pl
from jax.experimental.pallas import tpu as pltpu
from jax.sharding import PartitionSpec as P

BOTH = ("ctx", "mp")
PIECE = 128
NPIECES = 32
NSEQ = 8
MODES = 16
OWN = 32
TOKENS = 4096
BASE = NPIECES * 16
VROWS = BASE + NSEQ * 16
PARTS = 4
PART = 8192 // PARTS
CHUNK = 8
F32 = jnp.float32
BF16 = jnp.bfloat16


def lane_ids(shape):
    return lax.broadcasted_iota(jnp.int32, shape, 1)


def block_ids():
    return lane_ids((16, PIECE)) // OWN


def pack_kernel(a_ref, b_ref, c_ref, d_ref, o_ref, stage_ref, sem):
    refs = (a_ref, b_ref, c_ref, d_ref)

    def copy(a, part):
        cols = pl.ds(part * PART, PART)
        return pltpu.make_async_copy(
            refs[a].at[:, cols], stage_ref.at[a, :, cols], sem.at[a, part]
        )

    for part in range(PARTS):
        for a in range(4):
            copy(a, part).start()
    spot = block_ids()
    for part in range(PARTS):
        for a in range(4):
            copy(a, part).wait()

        def step(i, carry):
            at = part * (64 // PARTS) + i
            cols = pl.ds(pl.multiple_of(at * PIECE, PIECE), PIECE)
            turned = [
                pltpu.roll(stage_ref[a, :, cols].astype(F32), OWN * a, 1) if a
                else stage_ref[a, :, cols].astype(F32)
                for a in range(4)
            ]
            for k in range(4):
                tile = turned[(3 - k) % 4]
                for pos in range(3):
                    tile = jnp.where(spot == pos, turned[(pos - k) % 4], tile)
                o_ref[(4 * (at % 8) + k) * 8 + at // 8] = tile.astype(BF16)
            return carry

        lax.fori_loop(0, 64 // PARTS, step, 0, unroll=64 // PARTS)


def unpack_kernel(x_ref, a_ref, b_ref, c_ref, d_ref, stage_ref, sem):
    refs = (a_ref, b_ref, c_ref, d_ref)

    def copy(a, part):
        cols = pl.ds(part * PART, PART)
        return pltpu.make_async_copy(
            stage_ref.at[a, :, cols], refs[a].at[:, cols], sem.at[a, part]
        )

    spot = block_ids()
    for part in range(PARTS):

        def step(i, carry):
            at = part * (64 // PARTS) + i
            cols = pl.ds(pl.multiple_of(at * PIECE, PIECE), PIECE)
            tiles = [x_ref[(4 * (at % 8) + k) * 8 + at // 8].astype(F32) for k in range(4)]
            for a in range(4):
                mixed = tiles[(3 - a) % 4]
                for pos in range(3):
                    mixed = jnp.where(spot == pos, tiles[(pos - a) % 4], mixed)
                if a:
                    mixed = pltpu.roll(mixed, PIECE - OWN * a, 1)
                stage_ref[a, :, cols] = mixed.astype(BF16)
            return carry

        lax.fori_loop(0, 64 // PARTS, step, 0, unroll=64 // PARTS)
        for a in range(4):
            copy(a, part).start()
    for part in range(PARTS):
        for a in range(4):
            copy(a, part).wait()


def split(values):
    high = values.astype(BF16)
    return high, (values - high.astype(F32)).astype(BF16)


def dot3(left, right):
    def dot(a, b):
        return jnp.dot(a, b, preferred_element_type=F32)

    return dot(left[0], right[0]) + (dot(left[1], right[0]) + dot(left[0], right[1]))


(M_ONE, M_TWO, L_ONE, L_TWO, FIRST, TAIL, NOTBEG, NEXTCONT, WHOLE) = range(9)


def begins_of(lens_ref):
    begins = [jnp.int32(0)]
    for k in range(NSEQ):
        begins.append(begins[-1] + lens_ref[k])
    return begins


def prep_kernel(
    lens_ref, here_ref, taps_ref, res_ref, pole_ref, gain_ref,
    mask_ref, tapb_ref, tf_ref, tb_ref, we_ref, wh_ref, wr_ref, ws_ref,
    prep_ref,
):
    here = here_ref[0]
    begins = begins_of(lens_ref)

    shape = (NPIECES, PIECE)
    base = lax.broadcasted_iota(jnp.int32, shape, 0) * PIECE
    row = base + lane_ids(shape)

    def count(ids, upto=NSEQ):
        total = jnp.zeros(shape, jnp.int32)
        for k in range(upto):
            total = total + (begins[k] <= ids).astype(jnp.int32)
        return total

    def starts(ids):
        hit = ids == begins[0]
        for k in range(1, NSEQ + 1):
            hit = hit | (ids == begins[k])
        return hit

    own = count(row)
    at_first, at_last, before = count(base), count(base + PIECE - 1), count(base - 1)
    here_start, prior_start = starts(row), starts(row - 1)
    next_start, after_start = starts(row + 1), starts(row + 2)
    one = jnp.ones(shape, F32)
    zero = jnp.zeros(shape, F32)
    mask_ref[M_ONE] = jnp.where(here_start, zero, one)
    mask_ref[M_TWO] = jnp.where(here_start | prior_start, zero, one)
    mask_ref[L_ONE] = jnp.where(next_start, zero, one)
    mask_ref[L_TWO] = jnp.where(next_start | after_start, zero, one)
    mask_ref[FIRST] = jnp.where(own == at_first, one, zero)
    mask_ref[TAIL] = jnp.where(own == at_last, one, zero)
    mask_ref[NOTBEG] = jnp.where(at_first == before, one, zero)
    mask_ref[NEXTCONT] = jnp.where(starts(base + PIECE), zero, one)

    block = pl.ds(pl.multiple_of((here // 4) * 128, 128), 128)
    shift = lax.rem(128 - 32 * lax.rem(here, 4), 128)
    prep_ref[...] = jnp.zeros((PIECE, PIECE), F32)
    for a in range(3):
        for j in range(3):
            prep_ref[a * 3 + j : a * 3 + j + 1, :] = taps_ref[a, j : j + 1, block]
    prep_ref[9:10, :] = gain_ref[0:1, block]
    prep_ref[0:16, :] = pltpu.roll(prep_ref[0:16, :], shift, 1)
    prep_ref[16:18, 0:MODES] = pole_ref[pl.ds(2 * here, 2), :]
    prep_ref[24:26, 0:MODES] = res_ref[pl.ds(2 * here, 2), :]
    turned = prep_ref[...].T

    def column(rows, at):
        return jnp.broadcast_to(turned[0:rows, at : at + 1], (rows, PIECE))

    for j in range(3):
        for a in range(3):
            tapb_ref[j, a * OWN : (a + 1) * OWN, :] = column(OWN, a * 3 + j)
    tapb_ref[3, 0:OWN, :] = column(OWN, 9)
    tapb_ref[3, OWN:96, :] = jnp.zeros((64, PIECE), F32)
    pole = jnp.concatenate([column(MODES, 16), column(MODES, 17)], axis=0)
    residue = jnp.concatenate([column(MODES, 24), column(MODES, 25)], axis=0)
    weight = residue * jnp.sqrt(1.0 - pole * pole)
    lane = lane_ids((2 * MODES, PIECE))
    powers = jnp.ones((2 * MODES, PIECE), F32)
    falling = powers
    square = pole
    for bit in range(7):
        up = ((lane >> bit) & 1) == 1
        powers = jnp.where(up, powers * square, powers)
        falling = jnp.where(up, falling, falling * square)
        square = square * square
    rising = weight * (powers * pole)
    shrinking = weight * (falling * pole)
    taper = weight * powers

    sub_ids = lax.broadcasted_iota(jnp.int32, (PIECE, PIECE), 0)
    col_ids = lane_ids((PIECE, PIECE))
    tf_ref[...] = jnp.zeros(tf_ref.shape, BF16)
    tb_ref[...] = jnp.zeros(tb_ref.shape, BF16)
    wr_ref[...] = jnp.zeros(wr_ref.shape, BF16)
    ws_ref[...] = jnp.zeros(ws_ref.shape, BF16)
    for g in range(2):
        line = jnp.sum(taper[g * MODES : (g + 1) * MODES], axis=0, keepdims=True)
        spread = pltpu.roll(
            jnp.broadcast_to(line, (PIECE, PIECE)), 0, 1, stride=1, stride_axis=0
        )
        toeplitz = jnp.where(col_ids >= sub_ids, spread, 0.0)
        at = slice(g * PIECE, (g + 1) * PIECE)
        for part, tile in enumerate(split(toeplitz)):
            tf_ref[part, at, at] = tile
        for part, tile in enumerate(split(toeplitz.T)):
            tb_ref[part, at, at] = tile
        for ref, source in ((wr_ref, rising), (ws_ref, shrinking)):
            high, low = split(source[g * MODES : (g + 1) * MODES])
            ref[g * MODES : (g + 1) * MODES, at] = high
            ref[32 + g * MODES : 32 + (g + 1) * MODES, at] = high
            ref[64 + g * MODES : 64 + (g + 1) * MODES, at] = low
    blank = jnp.zeros((32, PIECE), F32)
    fall_cols = jnp.concatenate([falling, falling, falling, blank], axis=0).T
    power_cols = jnp.concatenate([powers, powers, powers, blank], axis=0).T
    group_zero = (col_ids & 16) == 0
    for ref, cols in ((we_ref, fall_cols), (wh_ref, power_cols)):
        for part, tile in enumerate(split(cols)):
            wide = tile.astype(F32)
            ref[part, 0:PIECE, :] = jnp.where(group_zero, wide, 0.0).astype(BF16)
            ref[part, PIECE:, :] = jnp.where(group_zero, 0.0, wide).astype(BF16)
    leap = fall_cols[0:1, :] * fall_cols[126:127, :]
    mask_ref[WHOLE] = leap * jnp.where(at_first == at_last, one, zero)

def store_lhs(ref, at, values):
    for part, tile in enumerate(split(values)):
        ref[part, pl.ds(at, 16), 0:PIECE] = tile[0:16]
        ref[part, pl.ds(at, 16), PIECE:] = tile[16:32]


def main_kernel(
    lens_ref, list_ref, here_ref, x_ref,
    mask_ref, tapb_ref, tf_ref, tb_ref, we_ref, wh_ref, wr_ref, ws_ref,
    y_ref, g_ref,
    xt_ref, feat_ref, z_ref, gu_ref,
    lzf_ref, lzt_ref, lgt_ref, lgf_ref,
    u_ref, gz_ref, e_ref, h_ref, gs_ref, ys_ref, acc_ref,
):
    begins = begins_of(lens_ref)
    turn = lax.rem(here_ref[0], 4)

    def place(pos):
        return pl.ds(pl.multiple_of(lax.rem(pos + turn, 4) * OWN, OWN), OWN)

    def unplace(pos):
        return pl.ds(pl.multiple_of(lax.rem(pos + 4 - turn, 4) * OWN, OWN), OWN)

    xt_ref[0] = jnp.zeros((PIECE, PIECE), F32)
    gs_ref[NPIECES] = jnp.zeros((96, PIECE), F32)
    acc_ref[...] = jnp.zeros(acc_ref.shape, F32)

    def turn_in(s, carry):
        tile = x_ref[pl.ds(s * 8, 8)].reshape(PIECE, PIECE).astype(F32).T
        p = list_ref[s] + 1
        for pos in range(4):
            xt_ref[p, unplace(pos), :] = tile[pos * OWN : (pos + 1) * OWN]
        return carry

    lax.fori_loop(0, NPIECES, turn_in, 0, unroll=CHUNK)

    lane = lane_ids((OWN, PIECE))

    def mask(which, p):
        return mask_ref[which, pl.ds(p, 1), :]

    def part(a):
        return slice(a * OWN, (a + 1) * OWN)

    def ahead(chunk, carry):
        skip = jnp.zeros((OWN, PIECE), F32)
        for i in range(CHUNK):
            p = chunk * CHUNK + i
            feats = []
            for a in range(3):
                x = xt_ref[p + 1, part(a), :]
                prior = xt_ref[p, part(a), :]
                x_one = pltpu.roll(jnp.where(lane == PIECE - 1, prior, x), 1, 1)
                x_two = pltpu.roll(jnp.where(lane >= PIECE - 2, prior, x), 2, 1)
                feat = (
                    tapb_ref[0, part(a), :] * x
                    + mask(M_ONE, p) * (tapb_ref[1, part(a), :] * x_one)
                    + mask(M_TWO, p) * (tapb_ref[2, part(a), :] * x_two)
                )
                feat_ref[p, part(a), :] = feat
                feats.append(feat)
            z = feats[1] * feats[2]
            gu = xt_ref[p + 1, part(3), :] * feats[0]
            z_ref[p] = z
            gu_ref[p] = gu
            skip = skip + gu * z
            first = mask(FIRST, p)
            tail = mask(TAIL, p)
            at = pl.multiple_of(p * 16, 16)
            store_lhs(lzf_ref, at, z * first)
            store_lhs(lzt_ref, at, z * tail)
            store_lhs(lgt_ref, at, gu * tail)
            store_lhs(lgf_ref, at, gu * first)
        acc_ref[0, part(3), :] += skip
        return carry

    lax.fori_loop(0, NPIECES // CHUNK, ahead, 0)

    line = lane_ids((1, PIECE))
    extras = []
    for k in range(1, NSEQ):
        p = begins[k] // PIECE
        rows = p * PIECE + line
        inner = lax.rem(begins[k], PIECE) != 0
        later = (rows >= begins[k]) & (rows < begins[k + 1]) & inner
        sooner = (rows >= begins[k - 1]) & (rows < begins[k]) & inner
        later = jnp.where(later, 1.0, 0.0)
        sooner = jnp.where(sooner, 1.0, 0.0)
        extras.append((p, later, sooner))
        store_lhs(lzf_ref, BASE + (k - 1) * 16, z_ref[p] * later)
        store_lhs(lgt_ref, BASE + (k - 1) * 16, gu_ref[p] * sooner)
    none = jnp.zeros((OWN, PIECE), F32)
    store_lhs(lzf_ref, VROWS - 16, none)
    store_lhs(lgt_ref, VROWS - 16, none)

    def both(ref):
        return ref[0], ref[1]

    e_ref[...] = dot3(both(lzt_ref), both(we_ref))
    h_ref[...] = dot3(both(lgf_ref), both(wh_ref))

    def scan(step, carry):
        state, back = carry
        p = step
        at = pl.ds(pl.multiple_of(p * 16, 16), 16)
        found = e_ref[at, :]
        state = state * mask(NOTBEG, p)
        e_ref[at, :] = state
        state = found + mask(WHOLE, p) * state
        p = NPIECES - 1 - step
        at = pl.ds(pl.multiple_of(p * 16, 16), 16)
        found = h_ref[at, :]
        back = back * mask(NEXTCONT, p)
        h_ref[at, :] = back
        back = found + mask(WHOLE, p) * back
        return state, back

    idle = jnp.zeros((16, PIECE), F32)
    lax.fori_loop(0, NPIECES, scan, (idle, idle), unroll=8)

    def three(states):
        high = states.astype(BF16).astype(F32)
        lane = lane_ids(states.shape)
        low = (lane >= 32) & (lane < 64)
        return jnp.where(low, states - high, high).astype(BF16)

    u_ref[...] = dot3(both(lzf_ref), both(tf_ref))
    gz_ref[...] = dot3(both(lgt_ref), both(tb_ref))
    u_ref[0:BASE, :] += jnp.dot(three(e_ref[...]), wr_ref[...], preferred_element_type=F32)
    gz_ref[0:BASE, :] += jnp.dot(three(h_ref[...]), ws_ref[...], preferred_element_type=F32)
    for k, (p, later, sooner) in enumerate(extras):
        at = pl.ds(pl.multiple_of(p * 16, 16), 16)
        more = slice(BASE + k * 16, BASE + (k + 1) * 16)
        for ref, kept in ((u_ref, later), (gz_ref, sooner)):
            for half in (slice(0, PIECE), slice(PIECE, 2 * PIECE)):
                ref[at, half] = jnp.where(kept > 0.0, ref[more, half], ref[at, half])

    def gradients(p, carry):
        at = pl.ds(pl.multiple_of(p * 16, 16), 16)
        gain = tapb_ref[3, 0:OWN, :]
        u = jnp.concatenate([u_ref[at, 0:PIECE], u_ref[at, PIECE:]], axis=0)
        gz = jnp.concatenate([gz_ref[at, 0:PIECE], gz_ref[at, PIECE:]], axis=0)
        filtered = u + gain * z_ref[p]
        gz = gz + gain * gu_ref[p]
        ys_ref[p, place(0), :] = feat_ref[p, part(0), :] * filtered
        gs_ref[p, part(0), :] = xt_ref[p + 1, part(3), :] * filtered
        gs_ref[p, part(1), :] = gz * feat_ref[p, part(2), :]
        gs_ref[p, part(2), :] = gz * feat_ref[p, part(1), :]
        return carry

    lax.fori_loop(0, NPIECES, gradients, 0, unroll=CHUNK)

    def behind(chunk, carry):
        for a in range(3):
            sums = [jnp.zeros((OWN, PIECE), F32) for _ in range(3)]
            for i in range(CHUNK):
                p = chunk * CHUNK + i
                grad = gs_ref[p, part(a), :]
                after = gs_ref[p + 1, part(a), :]
                x = xt_ref[p + 1, part(a), :]
                g_one = pltpu.roll(jnp.where(lane == 0, after, grad), PIECE - 1, 1)
                g_two = pltpu.roll(jnp.where(lane < 2, after, grad), PIECE - 2, 1)
                g_one = mask(L_ONE, p) * g_one
                g_two = mask(L_TWO, p) * g_two
                ys_ref[p, place(a + 1), :] = (
                    tapb_ref[0, part(a), :] * grad
                    + tapb_ref[1, part(a), :] * g_one
                    + tapb_ref[2, part(a), :] * g_two
                )
                for j, g in enumerate((grad, g_one, g_two)):
                    sums[j] = sums[j] + g * x
            for j in range(3):
                acc_ref[j, part(a), :] += sums[j]
        return carry

    lax.fori_loop(0, NPIECES // CHUNK, behind, 0)

    def turn_out(s, carry):
        tile = ys_ref[list_ref[s]].T.astype(BF16)
        y_ref[pl.ds(s * 8, 8)] = tile.reshape(8, 16, PIECE)
        return carry

    lax.fori_loop(0, NPIECES, turn_out, 0, unroll=CHUNK)
    norm = 1.0 / math.sqrt(TOKENS)
    g_ref[...] = jnp.zeros(g_ref.shape, F32)
    for j in range(3):
        g_ref[j : j + 1, :] = norm * jnp.sum(acc_ref[j].T, axis=0, keepdims=True)


def place_kernel(here_ref, parts_ref, taps_ref, skip_ref):
    here = here_ref[0]
    spot = lane_ids((8, PIECE)) // OWN
    for j in range(3):
        rows = []
        for k in range(4):
            picked = [parts_ref[(4 * q + k) ^ here, j : j + 1, :] for q in range(8)]
            rows.append(jnp.concatenate(picked, axis=0))
        for a in range(4 if j == 0 else 3):
            moved = [
                pltpu.roll(rows[k], ((k - a) % 4) * OWN, 1) if k != a else rows[k]
                for k in range(4)
            ]
            line = moved[3]
            for k in range(3):
                line = jnp.where(spot == k, moved[k], line)
            for q in range(8):
                cols = slice(q * PIECE, (q + 1) * PIECE)
                if a < 3:
                    taps_ref[a, j : j + 1, cols] = line[q : q + 1]
                else:
                    skip_ref[0:1, cols] = line[q : q + 1]


VM = pl.BlockSpec(memory_space=pltpu.VMEM)
SM = pl.BlockSpec(memory_space=pltpu.SMEM)
ANY = pl.BlockSpec(memory_space=pl.ANY)


def cost(flops, moved):
    return pl.CostEstimate(flops=flops, bytes_accessed=moved, transcendentals=0)


STAGE = [pltpu.VMEM((4, 16, 8192), BF16), pltpu.SemaphoreType.DMA((4, PARTS))]


def run_pack(*arrays):
    return pl.pallas_call(
        pack_kernel,
        out_shape=jax.ShapeDtypeStruct((256, 16, 128), BF16),
        in_specs=[ANY] * 4,
        out_specs=VM,
        scratch_shapes=STAGE,
        name="pack",
    )(*arrays)


def run_unpack(blocks):
    return pl.pallas_call(
        unpack_kernel,
        out_shape=[jax.ShapeDtypeStruct((16, 8192), BF16)] * 4,
        in_specs=[VM],
        out_specs=[ANY] * 4,
        scratch_shapes=STAGE,
        name="unpack",
    )(blocks)


def run_prep(lens, here, taps, residues, poles, gain):
    shapes = [
        ((9, NPIECES, PIECE), F32),
        ((4, 96, PIECE), F32),
        ((2, 256, 256), BF16),
        ((2, 256, 256), BF16),
        ((2, 256, PIECE), BF16),
        ((2, 256, PIECE), BF16),
        ((PIECE, 256), BF16),
        ((PIECE, 256), BF16),
    ]
    return pl.pallas_call(
        prep_kernel,
        out_shape=[jax.ShapeDtypeStruct(*shape) for shape in shapes],
        in_specs=[SM, SM, VM, VM, VM, VM],
        out_specs=[VM] * 8,
        scratch_shapes=[pltpu.VMEM((PIECE, PIECE), F32)],
        cost_estimate=cost(4_000_000, 1 << 20),
        name="prep",
    )(lens, here, taps, residues, poles, gain)


def run_main(lens, pieces, here, blocks, *prepared):
    scratch = [
        pltpu.VMEM((NPIECES + 1, PIECE, PIECE), F32),
        pltpu.VMEM((NPIECES, 96, PIECE), F32),
        pltpu.VMEM((NPIECES, OWN, PIECE), F32),
        pltpu.VMEM((NPIECES, OWN, PIECE), F32),
        pltpu.VMEM((2, VROWS, 256), BF16),
        pltpu.VMEM((2, BASE, 256), BF16),
        pltpu.VMEM((2, VROWS, 256), BF16),
        pltpu.VMEM((2, BASE, 256), BF16),
        pltpu.VMEM((VROWS, 256), F32),
        pltpu.VMEM((VROWS, 256), F32),
        pltpu.VMEM((BASE, PIECE), F32),
        pltpu.VMEM((BASE, PIECE), F32),
        pltpu.VMEM((NPIECES + 1, 96, PIECE), F32),
        pltpu.VMEM((NPIECES, PIECE, PIECE), F32),
        pltpu.VMEM((3, PIECE, PIECE), F32),
    ]
    return pl.pallas_call(
        main_kernel,
        out_shape=[
            jax.ShapeDtypeStruct((256, 16, 128), BF16),
            jax.ShapeDtypeStruct((8, 128), F32),
        ],
        in_specs=[SM, SM, SM] + [VM] * 9,
        out_specs=[VM, VM],
        scratch_shapes=scratch,
        compiler_params=pltpu.CompilerParams(vmem_limit_bytes=48 * 1024 * 1024),
        name="block",
    )(lens, pieces, here, blocks, *prepared)


def run_place(here, parts):
    return pl.pallas_call(
        place_kernel,
        out_shape=[
            jax.ShapeDtypeStruct((3, 3, 1024), F32),
            jax.ShapeDtypeStruct((1, 1024), F32),
        ],
        in_specs=[SM, VM],
        out_specs=[VM, VM],
        cost_estimate=cost(1_000_000, 1 << 17),
        name="place",
    )(here, parts)


def exchange(blocks):
    return lax.all_to_all(blocks, BOTH, split_axis=0, concat_axis=0, tiled=True)


def gather_sums(sums):
    held = sums[None]
    for bit in (1, 2, 4, 8, 16):
        pairs = [(i, i ^ bit) for i in range(32)]
        held = jnp.concatenate([held, lax.ppermute(held, "ctx", pairs)], axis=0)
    return held


def local(
    gate_rows,
    key_rows,
    value_rows,
    out_grad,
    conv_taps,
    filter_residues,
    filter_poles,
    skip_gain,
    seq_lengths,
    piece_list,
):
    here = lax.axis_index("ctx").astype(jnp.int32).reshape(1)
    blocks = exchange(run_pack(gate_rows, key_rows, value_rows, out_grad))
    prepared = run_prep(
        seq_lengths,
        here,
        conv_taps,
        filter_residues,
        filter_poles,
        skip_gain.reshape(1, -1),
    )
    results, sums = run_main(seq_lengths, piece_list, here, blocks, *prepared)
    outs = run_unpack(exchange(results))
    taps_grad, skip_grad = run_place(here, gather_sums(sums))
    return (*outs, taps_grad, skip_grad.reshape(1024))


def solution(mesh):
    rows = P(BOTH, None)
    return jax.shard_map(
        local,
        mesh=mesh,
        in_specs=(
            rows, rows, rows, rows,
            P(None, None, "mp"), P("mp", None), P("mp", None), P("mp"), P(), P(),
        ),
        out_specs=(rows, rows, rows, rows, P(None, None, "mp"), P("mp")),
        check_vma=False,
    )
```

```python
import math

import jax
import jax.numpy as jnp
from jax import lax
from jax.experimental import pallas as pl
from jax.experimental.pallas import tpu as pltpu
from jax.sharding import PartitionSpec as P

BOTH = ("ctx", "mp")
PIECE = 128
NPIECES = 32
NSEQ = 8
MODES = 16
OWN = 32
TOKENS = 4096
BASE = NPIECES * 16
VROWS = BASE + NSEQ * 16
PARTS = 4
PART = 8192 // PARTS
CHUNK = 8
MASKS = 9 * NPIECES
PLAN_ROWS = MASKS + 3 * 96 + OWN
T_AHEAD, T_BACK, C_AHEAD, C_BACK, E_BOTH = 0, 512, 1024, 1152, 1280
MAT_ROWS = 1792
LIMIT_MB = 48
F32 = jnp.float32
BF16 = jnp.bfloat16


def lane_ids(shape):
    return lax.broadcasted_iota(jnp.int32, shape, 1)


def block_ids():
    return lane_ids((16, PIECE)) // OWN


def pack_kernel(a_ref, b_ref, c_ref, d_ref, out_ref, stage_ref, o_ref, sem, out_sem):
    refs = (a_ref, b_ref, c_ref, d_ref)

    def copy(a, part):
        cols = pl.ds(part * PART, PART)
        return pltpu.make_async_copy(
            refs[a].at[:, cols], stage_ref.at[a, :, cols], sem.at[a, part]
        )

    def send(part):
        js = pl.ds(part * (8 // PARTS), 8 // PARTS)
        return pltpu.make_async_copy(o_ref.at[:, js], out_ref.at[:, js], out_sem.at[part])

    for part in range(PARTS):
        for a in range(4):
            copy(a, part).start()
    spot = block_ids()
    for part in range(PARTS):
        for a in range(4):
            copy(a, part).wait()

        def step(i, carry):
            at = part * (64 // PARTS) + i
            cols = pl.ds(pl.multiple_of(at * PIECE, PIECE), PIECE)
            turned = [
                pltpu.roll(stage_ref[a, :, cols].astype(F32), OWN * a, 1) if a
                else stage_ref[a, :, cols].astype(F32)
                for a in range(4)
            ]
            for k in range(4):
                tile = turned[(3 - k) % 4]
                for pos in range(3):
                    tile = jnp.where(spot == pos, turned[(pos - k) % 4], tile)
                o_ref[4 * (at % 8) + k, at // 8] = tile.astype(BF16)
            return carry

        lax.fori_loop(0, 64 // PARTS, step, 0, unroll=64 // PARTS)
        send(part).start()
    for part in range(PARTS):
        send(part).wait()


def place_sums(here, parts_ref, taps_ref, skip_ref):
    spot = lane_ids((8, PIECE)) // OWN

    def order(flip):
        return (flip >> 3) + 4 * (flip & 3) + 16 * ((flip >> 2) & 1)

    for j in range(3):
        rows = []
        for k in range(4):
            picked = [
                parts_ref[order((4 * q + k) ^ here), j : j + 1, :] for q in range(8)
            ]
            rows.append(jnp.concatenate(picked, axis=0))
        for a in range(4 if j == 0 else 3):
            moved = [
                pltpu.roll(rows[k], ((k - a) % 4) * OWN, 1) if k != a else rows[k]
                for k in range(4)
            ]
            line = moved[3]
            for k in range(3):
                line = jnp.where(spot == k, moved[k], line)
            for q in range(8):
                cols = slice(q * PIECE, (q + 1) * PIECE)
                if a < 3:
                    taps_ref[a, j : j + 1, cols] = line[q : q + 1]
                else:
                    skip_ref[0:1, cols] = line[q : q + 1]


def unpack_kernel(
    here_ref, x_ref, parts_ref, a_ref, b_ref, c_ref, d_ref, taps_ref, skip_ref,
    stage_ref, tapv_ref, skipv_ref, sem, small_sem,
):
    refs = (a_ref, b_ref, c_ref, d_ref)

    def copy(a, part):
        cols = pl.ds(part * PART, PART)
        return pltpu.make_async_copy(
            stage_ref.at[a, :, cols], refs[a].at[:, cols], sem.at[a, part]
        )

    spot = block_ids()
    for part in range(PARTS):

        def step(i, carry):
            at = part * (64 // PARTS) + i
            cols = pl.ds(pl.multiple_of(at * PIECE, PIECE), PIECE)
            tiles = [x_ref[4 * (at % 8) + k, at // 8].astype(F32) for k in range(4)]
            for a in range(4):
                mixed = tiles[(3 - a) % 4]
                for pos in range(3):
                    mixed = jnp.where(spot == pos, tiles[(pos - a) % 4], mixed)
                if a:
                    mixed = pltpu.roll(mixed, PIECE - OWN * a, 1)
                stage_ref[a, :, cols] = mixed.astype(BF16)
            return carry

        lax.fori_loop(0, 64 // PARTS, step, 0, unroll=64 // PARTS)
        for a in range(4):
            copy(a, part).start()
    place_sums(here_ref[0], parts_ref, tapv_ref, skipv_ref)
    taps_out = pltpu.make_async_copy(tapv_ref, taps_ref, small_sem.at[0])
    skip_out = pltpu.make_async_copy(skipv_ref, skip_ref, small_sem.at[1])
    taps_out.start()
    skip_out.start()
    for part in range(PARTS):
        for a in range(4):
            copy(a, part).wait()
    taps_out.wait()
    skip_out.wait()


def split(values):
    high = values.astype(BF16)
    return high, (values - high.astype(F32)).astype(BF16)


def dot3(left, right):
    def dot(a, b):
        return jnp.dot(a, b, preferred_element_type=F32)

    return dot(left[0], right[0]) + (dot(left[1], right[0]) + dot(left[0], right[1]))


(M_ONE, M_TWO, L_ONE, L_TWO, FIRST, TAIL, NOTBEG, NEXTCONT, WHOLE) = range(9)


def begins_of(lens_ref):
    begins = [jnp.int32(0)]
    for k in range(NSEQ):
        begins.append(begins[-1] + lens_ref[k])
    return begins


def prep_kernel(
    lens_ref, here_ref, taps_ref, res_ref, pole_ref, gain_ref,
    plan_ref, mats_ref,
    prep_ref,
):
    mask_ref = plan_ref.at[0:MASKS]
    tapb_ref = plan_ref.at[MASKS:]
    here = here_ref[0]
    begins = begins_of(lens_ref)

    shape = (NPIECES, PIECE)
    base = lax.broadcasted_iota(jnp.int32, shape, 0) * PIECE
    row = base + lane_ids(shape)

    def count(ids, upto=NSEQ):
        total = jnp.zeros(shape, jnp.int32)
        for k in range(upto):
            total = total + (begins[k] <= ids).astype(jnp.int32)
        return total

    def starts(ids):
        hit = ids == begins[0]
        for k in range(1, NSEQ + 1):
            hit = hit | (ids == begins[k])
        return hit

    own = count(row)
    at_first, at_last, before = count(base), count(base + PIECE - 1), count(base - 1)
    here_start, prior_start = starts(row), starts(row - 1)
    next_start, after_start = starts(row + 1), starts(row + 2)
    one = jnp.ones(shape, F32)
    zero = jnp.zeros(shape, F32)
    mask_ref[0:32, :] = jnp.where(here_start, zero, one)
    mask_ref[32:64, :] = jnp.where(here_start | prior_start, zero, one)
    mask_ref[64:96, :] = jnp.where(next_start, zero, one)
    mask_ref[96:128, :] = jnp.where(next_start | after_start, zero, one)
    mask_ref[128:160, :] = jnp.where(own == at_first, one, zero)
    mask_ref[160:192, :] = jnp.where(own == at_last, one, zero)
    mask_ref[192:224, :] = jnp.where(at_first == before, one, zero)
    mask_ref[224:256, :] = jnp.where(starts(base + PIECE), zero, one)

    block = pl.ds(pl.multiple_of((here // 4) * 128, 128), 128)
    shift = lax.rem(128 - 32 * lax.rem(here, 4), 128)
    prep_ref[...] = jnp.zeros((PIECE, PIECE), F32)
    for a in range(3):
        for j in range(3):
            prep_ref[a * 3 + j : a * 3 + j + 1, :] = taps_ref[a, j : j + 1, block]
    prep_ref[9:10, :] = gain_ref[0:1, block]
    prep_ref[0:16, :] = pltpu.roll(prep_ref[0:16, :], shift, 1)
    prep_ref[16:18, 0:MODES] = pole_ref[pl.ds(2 * here, 2), :]
    prep_ref[24:26, 0:MODES] = res_ref[pl.ds(2 * here, 2), :]
    turned = prep_ref[...].T

    def column(rows, at):
        return jnp.broadcast_to(turned[0:rows, at : at + 1], (rows, PIECE))

    for j in range(3):
        for a in range(3):
            tapb_ref[j * 96 + a * OWN : j * 96 + (a + 1) * OWN, :] = column(OWN, a * 3 + j)
    tapb_ref[288 : 288 + OWN, :] = column(OWN, 9)
    pole = jnp.concatenate([column(MODES, 16), column(MODES, 17)], axis=0)
    residue = jnp.concatenate([column(MODES, 24), column(MODES, 25)], axis=0)
    weight = residue * jnp.sqrt(1.0 - pole * pole)
    lane = lane_ids((2 * MODES, PIECE))
    powers = jnp.ones((2 * MODES, PIECE), F32)
    falling = powers
    square = pole
    for bit in range(7):
        up = ((lane >> bit) & 1) == 1
        powers = jnp.where(up, powers * square, powers)
        falling = jnp.where(up, falling, falling * square)
        square = square * square
    rising = weight * (powers * pole)
    shrinking = weight * (falling * pole)
    taper = weight * powers

    sub_ids = lax.broadcasted_iota(jnp.int32, (PIECE, PIECE), 0)
    col_ids = lane_ids((PIECE, PIECE))
    mats_ref[...] = jnp.zeros(mats_ref.shape, BF16)
    for g in range(2):
        line = jnp.sum(taper[g * MODES : (g + 1) * MODES], axis=0, keepdims=True)
        spread = pltpu.roll(
            jnp.broadcast_to(line, (PIECE, PIECE)), 0, 1, stride=1, stride_axis=0
        )
        toeplitz = jnp.where(col_ids >= sub_ids, spread, 0.0)
        at = slice(g * PIECE, (g + 1) * PIECE)
        for start, square_tile in ((T_AHEAD, toeplitz), (T_BACK, toeplitz.T)):
            for part, tile in enumerate(split(square_tile)):
                top = start + part * 256 + g * PIECE
                mats_ref[top : top + PIECE, at] = tile
        for start, source in ((C_AHEAD, rising), (C_BACK, shrinking)):
            high, low = split(source[g * MODES : (g + 1) * MODES])
            for top, tile in ((0, high), (32, high), (64, low)):
                top = start + top + g * MODES
                mats_ref[top : top + MODES, at] = tile
    blank = jnp.zeros((32, PIECE), F32)
    fall_cols = jnp.concatenate([falling, falling, falling, blank], axis=0).T
    power_cols = jnp.concatenate([powers, powers, powers, blank], axis=0).T
    group_zero = (col_ids & 16) == 0
    for half, cols in enumerate((fall_cols, power_cols)):
        at = slice(half * PIECE, (half + 1) * PIECE)
        for part, tile in enumerate(split(cols)):
            wide = tile.astype(F32)
            top = E_BOTH + part * 256
            mats_ref[top : top + PIECE, at] = jnp.where(group_zero, wide, 0.0).astype(BF16)
            mats_ref[top + PIECE : top + 256, at] = jnp.where(group_zero, 0.0, wide).astype(BF16)
    leap = fall_cols[0:1, :] * fall_cols[126:127, :]
    mask_ref[256:288, :] = leap * jnp.where(at_first == at_last, one, zero)

def store_lhs(ref, at, values):
    for part, tile in enumerate(split(values)):
        ref[part, pl.ds(at, 16), 0:PIECE] = tile[0:16]
        ref[part, pl.ds(at, 16), PIECE:] = tile[16:32]


def main_kernel(
    meta_ref, x_ref, plan_ref, mats_ref,
    out_ref, g_ref,
    inv_ref, xt_ref, feat_ref, z_ref, gu_ref, lzf_ref, lgt_ref,
    u_ref, gz_ref, e_ref, h_ref, gs_ref, ys_ref, y_ref, acc_ref, sem,
):
    lens_ref = meta_ref
    here = meta_ref[NSEQ + NPIECES]
    turn = lax.rem(here, 4)

    def place(pos):
        return pl.ds(pl.multiple_of(lax.rem(pos + turn, 4) * OWN, OWN), OWN)

    def unplace(pos):
        return pl.ds(pl.multiple_of(lax.rem(pos + 4 - turn, 4) * OWN, OWN), OWN)

    xt_ref[NPIECES] = jnp.zeros((PIECE, PIECE), F32)
    gs_ref[NPIECES] = jnp.zeros((96, PIECE), F32)
    acc_ref[...] = jnp.zeros(acc_ref.shape, F32)

    def turn_in(s, carry):
        tile = x_ref[pl.ds(s * 8, 8)].reshape(PIECE, PIECE)
        tile = tile.T.astype(F32)
        for pos in range(4):
            xt_ref[s, unplace(pos), :] = tile[pos * OWN : (pos + 1) * OWN]
        return carry

    lax.fori_loop(0, NPIECES, turn_in, 0, unroll=CHUNK)
    begins = begins_of(lens_ref)
    inv_ref[0] = NPIECES

    def invert(s, carry):
        inv_ref[meta_ref[NSEQ + s] + 1] = s
        return carry

    lax.fori_loop(0, NPIECES, invert, 0, unroll=4)

    lane = lane_ids((OWN, PIECE))

    def mask(which, p):
        return plan_ref[pl.ds(which * NPIECES + p, 1), :]

    def part(a):
        return slice(a * OWN, (a + 1) * OWN)

    def tap(j, a):
        top = MASKS + j * 96 + a * OWN
        return plan_ref[top : top + OWN, :]

    def mats(top, depth, cols=slice(0, 256)):
        return mats_ref[top : top + depth, cols], mats_ref[top + depth : top + 2 * depth, cols]

    def ahead(chunk, carry):
        skip = jnp.zeros((OWN, PIECE), F32)
        for i in range(CHUNK):
            p = chunk * CHUNK + i
            slot, before = inv_ref[p + 1], inv_ref[p]
            feats = []
            for a in range(3):
                x = xt_ref[slot, part(a), :]
                prior = xt_ref[before, part(a), :]
                x_one = pltpu.roll(jnp.where(lane == PIECE - 1, prior, x), 1, 1)
                x_two = pltpu.roll(jnp.where(lane >= PIECE - 2, prior, x), 2, 1)
                feat = (
                    tap(0, a) * x
                    + mask(M_ONE, p) * (tap(1, a) * x_one)
                    + mask(M_TWO, p) * (tap(2, a) * x_two)
                )
                feat_ref[p, part(a), :] = feat
                feats.append(feat)
            z = feats[1] * feats[2]
            gu = xt_ref[slot, part(3), :] * feats[0]
            z_ref[p] = z
            gu_ref[p] = gu
            skip = skip + gu * z
            first = mask(FIRST, p)
            tail = mask(TAIL, p)
            at = pl.multiple_of(p * 16, 16)
            store_lhs(lzf_ref, at, z * first)
            store_lhs(lgt_ref, at, gu * tail)
        acc_ref[0, part(3), :] += skip
        return carry

    lax.fori_loop(0, NPIECES // CHUNK, ahead, 0)

    line = lane_ids((1, PIECE))
    extras = []
    for k in range(1, NSEQ):
        p = begins[k] // PIECE
        rows = p * PIECE + line
        inner = lax.rem(begins[k], PIECE) != 0
        later = (rows >= begins[k]) & (rows < begins[k + 1]) & inner
        sooner = (rows >= begins[k - 1]) & (rows < begins[k]) & inner
        later = jnp.where(later, 1.0, 0.0)
        sooner = jnp.where(sooner, 1.0, 0.0)
        extras.append((p, later, sooner, inner))
        store_lhs(lzf_ref, BASE + (k - 1) * 16, z_ref[p] * later)
        store_lhs(lgt_ref, BASE + (k - 1) * 16, gu_ref[p] * sooner)
    none = jnp.zeros((OWN, PIECE), F32)
    store_lhs(lzf_ref, VROWS - 16, none)
    store_lhs(lgt_ref, VROWS - 16, none)

    def both(ref):
        return ref[0], ref[1]

    e_ref[...] = dot3(both(lzf_ref), mats(E_BOTH, 256, slice(0, PIECE)))
    h_ref[...] = dot3(both(lgt_ref), mats(E_BOTH, 256, slice(PIECE, 256)))
    for ref, ks in ((e_ref, range(NSEQ - 1)), (h_ref, range(NSEQ - 2, -1, -1))):
        for k in ks:
            p, _, _, inner = extras[k]
            at = pl.ds(pl.multiple_of(p * 16, 16), 16)
            ref[at, :] = jnp.where(inner, ref[BASE + k * 16 : BASE + (k + 1) * 16, :], ref[at, :])

    def scan(step, carry):
        state, back = carry
        p = step
        at = pl.ds(pl.multiple_of(p * 16, 16), 16)
        found = e_ref[at, :]
        state = state * mask(NOTBEG, p)
        e_ref[at, :] = state
        state = found + mask(WHOLE, p) * state
        p = NPIECES - 1 - step
        at = pl.ds(pl.multiple_of(p * 16, 16), 16)
        found = h_ref[at, :]
        back = back * mask(NEXTCONT, p)
        h_ref[at, :] = back
        back = found + mask(WHOLE, p) * back
        return state, back

    idle = jnp.zeros((16, PIECE), F32)
    lax.fori_loop(0, NPIECES, scan, (idle, idle), unroll=8)

    def three(states):
        high = states.astype(BF16).astype(F32)
        lane = lane_ids(states.shape)
        low = (lane >= 32) & (lane < 64)
        return jnp.where(low, states - high, high).astype(BF16)

    u_ref[...] = dot3(both(lzf_ref), mats(T_AHEAD, 256))
    gz_ref[...] = dot3(both(lgt_ref), mats(T_BACK, 256))
    u_ref[0:BASE, :] += jnp.dot(three(e_ref[0:BASE, :]), mats_ref[C_AHEAD : C_AHEAD + PIECE, :], preferred_element_type=F32)
    gz_ref[0:BASE, :] += jnp.dot(three(h_ref[0:BASE, :]), mats_ref[C_BACK : C_BACK + PIECE, :], preferred_element_type=F32)
    for k, (p, later, sooner, _) in enumerate(extras):
        at = pl.ds(pl.multiple_of(p * 16, 16), 16)
        more = slice(BASE + k * 16, BASE + (k + 1) * 16)
        for ref, kept in ((u_ref, later), (gz_ref, sooner)):
            for half in (slice(0, PIECE), slice(PIECE, 2 * PIECE)):
                ref[at, half] = jnp.where(kept > 0.0, ref[more, half], ref[at, half])

    def gradients(p, carry):
        at = pl.ds(pl.multiple_of(p * 16, 16), 16)
        gain = tap(3, 0)
        u = jnp.concatenate([u_ref[at, 0:PIECE], u_ref[at, PIECE:]], axis=0)
        gz = jnp.concatenate([gz_ref[at, 0:PIECE], gz_ref[at, PIECE:]], axis=0)
        filtered = u + gain * z_ref[p]
        gz = gz + gain * gu_ref[p]
        ys_ref[p, place(0), :] = (feat_ref[p, part(0), :] * filtered).astype(BF16)
        gs_ref[p, part(0), :] = xt_ref[inv_ref[p + 1], part(3), :] * filtered
        gs_ref[p, part(1), :] = gz * feat_ref[p, part(2), :]
        gs_ref[p, part(2), :] = gz * feat_ref[p, part(1), :]
        return carry

    lax.fori_loop(0, NPIECES, gradients, 0, unroll=CHUNK)

    def behind(chunk, carry):
        for a in range(3):
            sums = [jnp.zeros((OWN, PIECE), F32) for _ in range(3)]
            for i in range(CHUNK):
                p = chunk * CHUNK + i
                grad = gs_ref[p, part(a), :]
                after = gs_ref[p + 1, part(a), :]
                x = xt_ref[inv_ref[p + 1], part(a), :]
                g_one = pltpu.roll(jnp.where(lane == 0, after, grad), PIECE - 1, 1)
                g_two = pltpu.roll(jnp.where(lane < 2, after, grad), PIECE - 2, 1)
                g_one = mask(L_ONE, p) * g_one
                g_two = mask(L_TWO, p) * g_two
                back = (
                    tap(0, a) * grad
                    + tap(1, a) * g_one
                    + tap(2, a) * g_two
                )
                ys_ref[p, place(a + 1), :] = back.astype(BF16)
                for j, g in enumerate((grad, g_one, g_two)):
                    sums[j] = sums[j] + g * x
            for j in range(3):
                acc_ref[j, part(a), :] += sums[j]
        return carry

    lax.fori_loop(0, NPIECES // CHUNK, behind, 0)

    norm = 1.0 / math.sqrt(TOKENS)
    g_ref[...] = jnp.zeros(g_ref.shape, F32)
    for j in range(3):
        g_ref[j : j + 1, :] = norm * jnp.sum(acc_ref[j].T, axis=0, keepdims=True)

    def send(part):
        rows = pl.ds(part * 64, 64)
        return pltpu.make_async_copy(y_ref.at[rows], out_ref.at[rows], sem.at[part])

    for part in range(4):

        def turn_out(i, carry):
            s = part * 8 + i
            tile = ys_ref[meta_ref[NSEQ + s]].T
            y_ref[pl.ds(s * 8, 8)] = tile.reshape(8, 16, PIECE)
            return carry

        lax.fori_loop(0, 8, turn_out, 0, unroll=8)
        send(part).start()
    for part in range(4):
        send(part).wait()


VM = pl.BlockSpec(memory_space=pltpu.VMEM)
SM = pl.BlockSpec(memory_space=pltpu.SMEM)
ANY = pl.BlockSpec(memory_space=pl.ANY)


def cost(flops, moved):
    return pl.CostEstimate(flops=flops, bytes_accessed=moved, transcendentals=0)


def run_pack(*arrays):
    blocks = pl.pallas_call(
        pack_kernel,
        out_shape=jax.ShapeDtypeStruct((32, 8, 16, 128), BF16),
        in_specs=[ANY] * 4,
        out_specs=ANY,
        scratch_shapes=[
            pltpu.VMEM((4, 16, 8192), BF16),
            pltpu.VMEM((32, 8, 16, 128), BF16),
            pltpu.SemaphoreType.DMA((4, PARTS)),
            pltpu.SemaphoreType.DMA((PARTS,)),
        ],
        name="pack",
    )(*arrays)
    return blocks.reshape(256, 16, 128)


def run_unpack(here, blocks, sums):
    return pl.pallas_call(
        unpack_kernel,
        out_shape=[jax.ShapeDtypeStruct((16, 8192), BF16)] * 4
        + [
            jax.ShapeDtypeStruct((3, 3, 1024), F32),
            jax.ShapeDtypeStruct((1, 1024), F32),
        ],
        in_specs=[SM, VM, VM],
        out_specs=[ANY] * 6,
        scratch_shapes=[
            pltpu.VMEM((4, 16, 8192), BF16),
            pltpu.VMEM((3, 3, 1024), F32),
            pltpu.VMEM((1, 1024), F32),
            pltpu.SemaphoreType.DMA((4, PARTS)),
            pltpu.SemaphoreType.DMA((2,)),
        ],
        compiler_params=pltpu.CompilerParams(vmem_limit_bytes=24 << 20),
        name="unpack",
    )(here, blocks.reshape(32, 8, 16, 128), sums)


def run_prep(lens, here, taps, residues, poles, gain):
    shapes = [((PLAN_ROWS, PIECE), F32), ((MAT_ROWS, 256), BF16)]
    return pl.pallas_call(
        prep_kernel,
        out_shape=[jax.ShapeDtypeStruct(*shape) for shape in shapes],
        in_specs=[SM, SM, VM, VM, VM, VM],
        out_specs=[VM] * 2,
        scratch_shapes=[pltpu.VMEM((PIECE, PIECE), F32)],
        cost_estimate=cost(4_000_000, 1 << 20),
        name="prep",
    )(lens, here, taps, residues, poles, gain)


def run_main(meta, blocks, plan, mats):
    scratch = [
        pltpu.SMEM((NPIECES + 1,), jnp.int32),
        pltpu.VMEM((NPIECES + 1, PIECE, PIECE), F32),
        pltpu.VMEM((NPIECES, 96, PIECE), F32),
        pltpu.VMEM((NPIECES, OWN, PIECE), F32),
        pltpu.VMEM((NPIECES, OWN, PIECE), F32),
        pltpu.VMEM((2, VROWS, 256), BF16),
        pltpu.VMEM((2, VROWS, 256), BF16),
        pltpu.VMEM((VROWS, 256), F32),
        pltpu.VMEM((VROWS, 256), F32),
        pltpu.VMEM((VROWS, PIECE), F32),
        pltpu.VMEM((VROWS, PIECE), F32),
        pltpu.VMEM((NPIECES + 1, 96, PIECE), F32),
        pltpu.VMEM((NPIECES, PIECE, PIECE), BF16),
        pltpu.VMEM((256, 16, 128), BF16),
        pltpu.VMEM((3, PIECE, PIECE), F32),
        pltpu.SemaphoreType.DMA((4,)),
    ]
    return pl.pallas_call(
        main_kernel,
        out_shape=[
            jax.ShapeDtypeStruct((256, 16, 128), BF16),
            jax.ShapeDtypeStruct((8, 128), F32),
        ],
        in_specs=[SM, VM, VM, VM],
        out_specs=[ANY, VM],
        scratch_shapes=scratch,
        compiler_params=pltpu.CompilerParams(vmem_limit_bytes=LIMIT_MB << 20),
        name="block",
    )(meta, blocks, plan, mats)


def exchange(blocks):
    return lax.all_to_all(blocks, BOTH, split_axis=0, concat_axis=0, tiled=True)


def gather_sums(sums):
    held = sums[None]
    for flips in ((8, 16, 24), (1, 2, 3), (4,)):
        got = [held]
        for flip in flips:
            pairs = [(i, i ^ flip) for i in range(32)]
            got.append(lax.ppermute(held, "ctx", pairs))
        held = jnp.concatenate(got, axis=0)
    return held


def local(
    gate_rows,
    key_rows,
    value_rows,
    out_grad,
    conv_taps,
    filter_residues,
    filter_poles,
    skip_gain,
    seq_lengths,
    piece_list,
):
    here = lax.axis_index("ctx").astype(jnp.int32).reshape(1)
    blocks = exchange(run_pack(gate_rows, key_rows, value_rows, out_grad))
    plan, mats = run_prep(
        seq_lengths,
        here,
        conv_taps,
        filter_residues,
        filter_poles,
        skip_gain.reshape(1, -1),
    )
    plan = jnp.pad(plan, ((0, 8), (0, 0)))
    mats = jnp.pad(mats, ((0, 16), (0, 0)))
    meta = jnp.concatenate([seq_lengths, piece_list, here])
    results, sums = run_main(meta, blocks, plan, mats)
    *outs, taps_grad, skip_grad = run_unpack(here, exchange(results), gather_sums(sums))
    return (*outs, taps_grad, skip_grad.reshape(1024))


def solution(mesh):
    rows = P(BOTH, None)
    return jax.shard_map(
        local,
        mesh=mesh,
        in_specs=(
            rows, rows, rows, rows,
            P(None, None, "mp"), P("mp", None), P("mp", None), P("mp"), P(), P(),
        ),
        out_specs=(rows, rows, rows, rows, P(None, None, "mp"), P("mp")),
        check_vma=False,
    )
```

```python
import math

import jax
import jax.numpy as jnp
from jax import lax
from jax.experimental import pallas as pl
from jax.experimental.pallas import tpu as pltpu
from jax.sharding import PartitionSpec as P

BOTH = ("ctx", "mp")
PIECE = 128
NPIECES = 32
NSEQ = 8
MODES = 16
OWN = 32
TOKENS = 4096
BASE = NPIECES * 16
VROWS = BASE + NSEQ * 16
PARTS = 4
PART = 8192 // PARTS
CHUNK = 8
MASKS = 9 * NPIECES
PLAN_ROWS = MASKS + 3 * 96 + OWN
T_AHEAD, T_BACK, C_AHEAD, C_BACK, E_BOTH = 0, 512, 1024, 1152, 1280
MAT_ROWS = 1792
LIMIT_MB = 48
F32 = jnp.float32
BF16 = jnp.bfloat16


def lane_ids(shape):
    return lax.broadcasted_iota(jnp.int32, shape, 1)


def block_ids():
    return lane_ids((16, PIECE)) // OWN


def pack_kernel(a_ref, b_ref, c_ref, d_ref, out_ref, stage_ref, o_ref, sem, out_sem):
    refs = (a_ref, b_ref, c_ref, d_ref)

    def copy(a, part):
        cols = pl.ds(part * PART, PART)
        return pltpu.make_async_copy(
            refs[a].at[:, cols], stage_ref.at[a, :, cols], sem.at[a, part]
        )

    def send(part):
        js = pl.ds(part * (8 // PARTS), 8 // PARTS)
        return pltpu.make_async_copy(o_ref.at[:, js], out_ref.at[:, js], out_sem.at[part])

    for part in range(PARTS):
        for a in range(4):
            copy(a, part).start()
    spot = block_ids()
    for part in range(PARTS):
        for a in range(4):
            copy(a, part).wait()

        def step(i, carry):
            at = part * (64 // PARTS) + i
            cols = pl.ds(pl.multiple_of(at * PIECE, PIECE), PIECE)
            turned = [
                pltpu.roll(stage_ref[a, :, cols].astype(F32), OWN * a, 1) if a
                else stage_ref[a, :, cols].astype(F32)
                for a in range(4)
            ]
            for k in range(4):
                tile = turned[(3 - k) % 4]
                for pos in range(3):
                    tile = jnp.where(spot == pos, turned[(pos - k) % 4], tile)
                o_ref[4 * (at % 8) + k, at // 8] = tile.astype(BF16)
            return carry

        lax.fori_loop(0, 64 // PARTS, step, 0, unroll=64 // PARTS)
        send(part).start()
    for part in range(PARTS):
        send(part).wait()


def place_sums(here, parts_ref, taps_ref, skip_ref):
    spot = lane_ids((8, PIECE)) // OWN

    def order(flip):
        return (flip >> 3) + 4 * (flip & 3) + 16 * ((flip >> 2) & 1)

    for j in range(3):
        rows = []
        for k in range(4):
            picked = [
                parts_ref[order((4 * q + k) ^ here), j : j + 1, :] for q in range(8)
            ]
            rows.append(jnp.concatenate(picked, axis=0))
        for a in range(4 if j == 0 else 3):
            moved = [
                pltpu.roll(rows[k], ((k - a) % 4) * OWN, 1) if k != a else rows[k]
                for k in range(4)
            ]
            line = moved[3]
            for k in range(3):
                line = jnp.where(spot == k, moved[k], line)
            for q in range(8):
                cols = slice(q * PIECE, (q + 1) * PIECE)
                if a < 3:
                    taps_ref[a, j : j + 1, cols] = line[q : q + 1]
                else:
                    skip_ref[0:1, cols] = line[q : q + 1]


def unpack_kernel(
    here_ref, x_ref, parts_ref, a_ref, b_ref, c_ref, d_ref, taps_ref, skip_ref,
    stage_ref, tapv_ref, skipv_ref, sem, small_sem,
):
    refs = (a_ref, b_ref, c_ref, d_ref)

    def copy(a, part):
        cols = pl.ds(part * PART, PART)
        return pltpu.make_async_copy(
            stage_ref.at[a, :, cols], refs[a].at[:, cols], sem.at[a, part]
        )

    spot = block_ids()
    for part in range(PARTS):

        def step(i, carry):
            at = part * (64 // PARTS) + i
            cols = pl.ds(pl.multiple_of(at * PIECE, PIECE), PIECE)
            tiles = [x_ref[4 * (at % 8) + k, at // 8].astype(F32) for k in range(4)]
            for a in range(4):
                mixed = tiles[(3 - a) % 4]
                for pos in range(3):
                    mixed = jnp.where(spot == pos, tiles[(pos - a) % 4], mixed)
                if a:
                    mixed = pltpu.roll(mixed, PIECE - OWN * a, 1)
                stage_ref[a, :, cols] = mixed.astype(BF16)
            return carry

        lax.fori_loop(0, 64 // PARTS, step, 0, unroll=64 // PARTS)
        for a in range(4):
            copy(a, part).start()
    place_sums(here_ref[0], parts_ref, tapv_ref, skipv_ref)
    taps_out = pltpu.make_async_copy(tapv_ref, taps_ref, small_sem.at[0])
    skip_out = pltpu.make_async_copy(skipv_ref, skip_ref, small_sem.at[1])
    taps_out.start()
    skip_out.start()
    for part in range(PARTS):
        for a in range(4):
            copy(a, part).wait()
    taps_out.wait()
    skip_out.wait()


def split(values):
    high = values.astype(BF16)
    return high, (values - high.astype(F32)).astype(BF16)


def dot3(left, right):
    left = jnp.concatenate([left[0], left[1], left[0]], axis=1)
    right = jnp.concatenate([right[0], right[0], right[1]], axis=0)
    return jnp.dot(left, right, preferred_element_type=F32)


(M_ONE, M_TWO, L_ONE, L_TWO, FIRST, TAIL, NOTBEG, NEXTCONT, WHOLE) = range(9)


def begins_of(lens_ref):
    begins = [jnp.int32(0)]
    for k in range(NSEQ):
        begins.append(begins[-1] + lens_ref[k])
    return begins


def prep_kernel(
    lens_ref, here_ref, taps_ref, res_ref, pole_ref, gain_ref,
    plan_ref, mats_ref,
    prep_ref,
):
    mask_ref = plan_ref.at[0:MASKS]
    tapb_ref = plan_ref.at[MASKS:]
    here = here_ref[0]
    begins = begins_of(lens_ref)

    shape = (NPIECES, PIECE)
    base = lax.broadcasted_iota(jnp.int32, shape, 0) * PIECE
    row = base + lane_ids(shape)

    def count(ids, upto=NSEQ):
        total = jnp.zeros(shape, jnp.int32)
        for k in range(upto):
            total = total + (begins[k] <= ids).astype(jnp.int32)
        return total

    def starts(ids):
        hit = ids == begins[0]
        for k in range(1, NSEQ + 1):
            hit = hit | (ids == begins[k])
        return hit

    own = count(row)
    at_first, at_last, before = count(base), count(base + PIECE - 1), count(base - 1)
    here_start, prior_start = starts(row), starts(row - 1)
    next_start, after_start = starts(row + 1), starts(row + 2)
    one = jnp.ones(shape, F32)
    zero = jnp.zeros(shape, F32)
    mask_ref[0:32, :] = jnp.where(here_start, zero, one)
    mask_ref[32:64, :] = jnp.where(here_start | prior_start, zero, one)
    mask_ref[64:96, :] = jnp.where(next_start, zero, one)
    mask_ref[96:128, :] = jnp.where(next_start | after_start, zero, one)
    mask_ref[128:160, :] = jnp.where(own == at_first, one, zero)
    mask_ref[160:192, :] = jnp.where(own == at_last, one, zero)
    mask_ref[192:224, :] = jnp.where(at_first == before, one, zero)
    mask_ref[224:256, :] = jnp.where(starts(base + PIECE), zero, one)

    block = pl.ds(pl.multiple_of((here // 4) * 128, 128), 128)
    shift = lax.rem(128 - 32 * lax.rem(here, 4), 128)
    prep_ref[...] = jnp.zeros((PIECE, PIECE), F32)
    for a in range(3):
        for j in range(3):
            prep_ref[a * 3 + j : a * 3 + j + 1, :] = taps_ref[a, j : j + 1, block]
    prep_ref[9:10, :] = gain_ref[0:1, block]
    prep_ref[0:16, :] = pltpu.roll(prep_ref[0:16, :], shift, 1)
    prep_ref[16:18, 0:MODES] = pole_ref[pl.ds(2 * here, 2), :]
    prep_ref[24:26, 0:MODES] = res_ref[pl.ds(2 * here, 2), :]
    turned = prep_ref[...].T

    def column(rows, at):
        return jnp.broadcast_to(turned[0:rows, at : at + 1], (rows, PIECE))

    for j in range(3):
        for a in range(3):
            tapb_ref[j * 96 + a * OWN : j * 96 + (a + 1) * OWN, :] = column(OWN, a * 3 + j)
    tapb_ref[288 : 288 + OWN, :] = column(OWN, 9)
    pole = jnp.concatenate([column(MODES, 16), column(MODES, 17)], axis=0)
    residue = jnp.concatenate([column(MODES, 24), column(MODES, 25)], axis=0)
    weight = residue * jnp.sqrt(1.0 - pole * pole)
    lane = lane_ids((2 * MODES, PIECE))
    powers = jnp.ones((2 * MODES, PIECE), F32)
    falling = powers
    square = pole
    for bit in range(7):
        up = ((lane >> bit) & 1) == 1
        powers = jnp.where(up, powers * square, powers)
        falling = jnp.where(up, falling, falling * square)
        square = square * square
    rising = weight * (powers * pole)
    shrinking = weight * (falling * pole)
    taper = weight * powers

    sub_ids = lax.broadcasted_iota(jnp.int32, (PIECE, PIECE), 0)
    col_ids = lane_ids((PIECE, PIECE))
    mats_ref[...] = jnp.zeros(mats_ref.shape, BF16)
    for g in range(2):
        line = jnp.sum(taper[g * MODES : (g + 1) * MODES], axis=0, keepdims=True)
        spread = pltpu.roll(
            jnp.broadcast_to(line, (PIECE, PIECE)), 0, 1, stride=1, stride_axis=0
        )
        toeplitz = jnp.where(col_ids >= sub_ids, spread, 0.0)
        at = slice(g * PIECE, (g + 1) * PIECE)
        for start, square_tile in ((T_AHEAD, toeplitz), (T_BACK, toeplitz.T)):
            for part, tile in enumerate(split(square_tile)):
                top = start + part * 256 + g * PIECE
                mats_ref[top : top + PIECE, at] = tile
        for start, source in ((C_AHEAD, rising), (C_BACK, shrinking)):
            high, low = split(source[g * MODES : (g + 1) * MODES])
            for top, tile in ((0, high), (32, high), (64, low)):
                top = start + top + g * MODES
                mats_ref[top : top + MODES, at] = tile
    blank = jnp.zeros((32, PIECE), F32)
    fall_cols = jnp.concatenate([falling, falling, falling, blank], axis=0).T
    power_cols = jnp.concatenate([powers, powers, powers, blank], axis=0).T
    group_zero = (col_ids & 16) == 0
    for half, cols in enumerate((fall_cols, power_cols)):
        at = slice(half * PIECE, (half + 1) * PIECE)
        for part, tile in enumerate(split(cols)):
            wide = tile.astype(F32)
            top = E_BOTH + part * 256
            mats_ref[top : top + PIECE, at] = jnp.where(group_zero, wide, 0.0).astype(BF16)
            mats_ref[top + PIECE : top + 256, at] = jnp.where(group_zero, 0.0, wide).astype(BF16)
    leap = fall_cols[0:1, :] * fall_cols[126:127, :]
    mask_ref[256:288, :] = leap * jnp.where(at_first == at_last, one, zero)

def store_lhs(ref, at, values):
    for part, tile in enumerate(split(values)):
        ref[part, pl.ds(at, 16), 0:PIECE] = tile[0:16]
        ref[part, pl.ds(at, 16), PIECE:] = tile[16:32]


def unrolled(count, body, carry):
    for i in range(count):
        carry = body(i, carry)
    return carry


def main_kernel(
    meta_ref, x_ref, plan_ref, mats_ref,
    out_ref, g_ref,
    inv_ref, xt_ref, feat_ref, z_ref, gu_ref, lzf_ref, lgt_ref,
    u_ref, gz_ref, e_ref, h_ref, gs_ref, ys_ref, y_ref, acc_ref, sem,
):
    lens_ref = meta_ref
    here = meta_ref[NSEQ + NPIECES]
    turn = lax.rem(here, 4)

    def place(pos):
        return pl.ds(pl.multiple_of(lax.rem(pos + turn, 4) * OWN, OWN), OWN)

    def unplace(pos):
        return pl.ds(pl.multiple_of(lax.rem(pos + 4 - turn, 4) * OWN, OWN), OWN)

    xt_ref[NPIECES] = jnp.zeros((PIECE, PIECE), F32)
    gs_ref[NPIECES] = jnp.zeros((96, PIECE), F32)
    acc_ref[...] = jnp.zeros(acc_ref.shape, F32)

    def turn_in(s, carry):
        tile = x_ref[pl.ds(s * 8, 8)].reshape(PIECE, PIECE)
        tile = tile.T.astype(F32)
        for pos in range(4):
            xt_ref[s, unplace(pos), :] = tile[pos * OWN : (pos + 1) * OWN]
        return carry

    unrolled(NPIECES, turn_in, 0)
    begins = begins_of(lens_ref)
    inv_ref[0] = NPIECES

    def invert(s, carry):
        inv_ref[meta_ref[NSEQ + s] + 1] = s
        return carry

    lax.fori_loop(0, NPIECES, invert, 0, unroll=4)

    lane = lane_ids((OWN, PIECE))

    def mask(which, p):
        return plan_ref[pl.ds(which * NPIECES + p, 1), :]

    def part(a):
        return slice(a * OWN, (a + 1) * OWN)

    def tap(j, a):
        top = MASKS + j * 96 + a * OWN
        return plan_ref[top : top + OWN, :]

    def mats(top, depth, cols=slice(0, 256)):
        return mats_ref[top : top + depth, cols], mats_ref[top + depth : top + 2 * depth, cols]

    def ahead(chunk, carry):
        pieces = range(chunk * CHUNK, (chunk + 1) * CHUNK)
        slots = [inv_ref[p] for p in range(chunk * CHUNK, (chunk + 1) * CHUNK + 1)]
        for a in range(3):
            taps = [tap(j, a) for j in range(3)]
            prior = xt_ref[slots[0], part(a), :]
            for i, p in enumerate(pieces):
                x = xt_ref[slots[i + 1], part(a), :]
                x_one = pltpu.roll(jnp.where(lane == PIECE - 1, prior, x), 1, 1)
                x_two = pltpu.roll(jnp.where(lane >= PIECE - 2, prior, x), 2, 1)
                feat_ref[p, part(a), :] = (
                    taps[0] * x
                    + mask(M_ONE, p) * (taps[1] * x_one)
                    + mask(M_TWO, p) * (taps[2] * x_two)
                )
                prior = x
        skip = jnp.zeros((OWN, PIECE), F32)
        for i, p in enumerate(pieces):
            z = feat_ref[p, part(1), :] * feat_ref[p, part(2), :]
            gu = xt_ref[slots[i + 1], part(3), :] * feat_ref[p, part(0), :]
            z_ref[p] = z
            gu_ref[p] = gu
            skip = skip + gu * z
            store_lhs(lzf_ref, p * 16, z * mask(FIRST, p))
            store_lhs(lgt_ref, p * 16, gu * mask(TAIL, p))
        acc_ref[0, part(3), :] += skip
        return carry

    unrolled(NPIECES // CHUNK, ahead, 0)

    line = lane_ids((1, PIECE))
    extras = []
    for k in range(1, NSEQ):
        p = begins[k] // PIECE
        rows = p * PIECE + line
        inner = lax.rem(begins[k], PIECE) != 0
        later = (rows >= begins[k]) & (rows < begins[k + 1]) & inner
        sooner = (rows >= begins[k - 1]) & (rows < begins[k]) & inner
        later = jnp.where(later, 1.0, 0.0)
        sooner = jnp.where(sooner, 1.0, 0.0)
        extras.append((p, later, sooner, inner))
        store_lhs(lzf_ref, BASE + (k - 1) * 16, z_ref[p] * later)
        store_lhs(lgt_ref, BASE + (k - 1) * 16, gu_ref[p] * sooner)
    none = jnp.zeros((OWN, PIECE), F32)
    store_lhs(lzf_ref, VROWS - 16, none)
    store_lhs(lgt_ref, VROWS - 16, none)

    def both(ref):
        return ref[0], ref[1]

    e_ref[...] = dot3(both(lzf_ref), mats(E_BOTH, 256, slice(0, PIECE)))
    h_ref[...] = dot3(both(lgt_ref), mats(E_BOTH, 256, slice(PIECE, 256)))
    for ref, ks in ((e_ref, range(NSEQ - 1)), (h_ref, range(NSEQ - 2, -1, -1))):
        for k in ks:
            p, _, _, inner = extras[k]
            at = pl.ds(pl.multiple_of(p * 16, 16), 16)
            ref[at, :] = jnp.where(inner, ref[BASE + k * 16 : BASE + (k + 1) * 16, :], ref[at, :])

    def scan(step, carry):
        state, back = carry
        p = step
        at = pl.ds(p * 16, 16)
        found = e_ref[at, :]
        state = state * mask(NOTBEG, p)
        e_ref[at, :] = state
        state = found + mask(WHOLE, p) * state
        p = NPIECES - 1 - step
        at = pl.ds(p * 16, 16)
        found = h_ref[at, :]
        back = back * mask(NEXTCONT, p)
        h_ref[at, :] = back
        back = found + mask(WHOLE, p) * back
        return state, back

    idle = jnp.zeros((16, PIECE), F32)
    unrolled(NPIECES, scan, (idle, idle))

    def three(states):
        high = states.astype(BF16).astype(F32)
        lane = lane_ids(states.shape)
        low = (lane >= 32) & (lane < 64)
        return jnp.where(low, states - high, high).astype(BF16)

    u_ref[...] = dot3(both(lzf_ref), mats(T_AHEAD, 256))
    gz_ref[...] = dot3(both(lgt_ref), mats(T_BACK, 256))
    u_ref[0:BASE, :] += jnp.dot(three(e_ref[0:BASE, :]), mats_ref[C_AHEAD : C_AHEAD + PIECE, :], preferred_element_type=F32)
    gz_ref[0:BASE, :] += jnp.dot(three(h_ref[0:BASE, :]), mats_ref[C_BACK : C_BACK + PIECE, :], preferred_element_type=F32)
    for k, (p, later, sooner, _) in enumerate(extras):
        at = pl.ds(pl.multiple_of(p * 16, 16), 16)
        more = slice(BASE + k * 16, BASE + (k + 1) * 16)
        for ref, kept in ((u_ref, later), (gz_ref, sooner)):
            for half in (slice(0, PIECE), slice(PIECE, 2 * PIECE)):
                ref[at, half] = jnp.where(kept > 0.0, ref[more, half], ref[at, half])

    def gradients(p, carry):
        at = pl.ds(p * 16, 16)
        gain = tap(3, 0)
        u = jnp.concatenate([u_ref[at, 0:PIECE], u_ref[at, PIECE:]], axis=0)
        gz = jnp.concatenate([gz_ref[at, 0:PIECE], gz_ref[at, PIECE:]], axis=0)
        filtered = u + gain * z_ref[p]
        gz = gz + gain * gu_ref[p]
        ys_ref[p, place(0), :] = (feat_ref[p, part(0), :] * filtered).astype(BF16)
        gs_ref[p, part(0), :] = xt_ref[inv_ref[p + 1], part(3), :] * filtered
        gs_ref[p, part(1), :] = gz * feat_ref[p, part(2), :]
        gs_ref[p, part(2), :] = gz * feat_ref[p, part(1), :]
        return carry

    unrolled(NPIECES, gradients, 0)

    def behind(chunk, carry):
        for a in range(3):
            taps = [tap(j, a) for j in range(3)]
            sums = [jnp.zeros((OWN, PIECE), F32) for _ in range(3)]
            after = gs_ref[(chunk + 1) * CHUNK, part(a), :]
            for p in reversed(range(chunk * CHUNK, (chunk + 1) * CHUNK)):
                grad = gs_ref[p, part(a), :]
                x = xt_ref[inv_ref[p + 1], part(a), :]
                g_one = pltpu.roll(jnp.where(lane == 0, after, grad), PIECE - 1, 1)
                g_two = pltpu.roll(jnp.where(lane < 2, after, grad), PIECE - 2, 1)
                g_one = mask(L_ONE, p) * g_one
                g_two = mask(L_TWO, p) * g_two
                back = taps[0] * grad + taps[1] * g_one + taps[2] * g_two
                ys_ref[p, place(a + 1), :] = back.astype(BF16)
                for j, g in enumerate((grad, g_one, g_two)):
                    sums[j] = sums[j] + g * x
                after = grad
            for j in range(3):
                acc_ref[j, part(a), :] += sums[j]
        return carry

    unrolled(NPIECES // CHUNK, behind, 0)

    def send(part):
        rows = pl.ds(part * 64, 64)
        return pltpu.make_async_copy(y_ref.at[rows], out_ref.at[rows], sem.at[part])

    for part in range(4):

        def turn_out(i, carry):
            s = part * 8 + i
            tile = ys_ref[meta_ref[NSEQ + s]].T
            y_ref[pl.ds(s * 8, 8)] = tile.reshape(8, 16, PIECE)
            return carry

        unrolled(8, turn_out, 0)
        send(part).start()
    norm = 1.0 / math.sqrt(TOKENS)
    g_ref[3:4, :] = jnp.zeros((1, PIECE), F32)
    for j in range(3):
        g_ref[j : j + 1, :] = norm * jnp.sum(acc_ref[j].T, axis=0, keepdims=True)
    for part in range(4):
        send(part).wait()


VM = pl.BlockSpec(memory_space=pltpu.VMEM)
SM = pl.BlockSpec(memory_space=pltpu.SMEM)
ANY = pl.BlockSpec(memory_space=pl.ANY)


def cost(flops, moved):
    return pl.CostEstimate(flops=flops, bytes_accessed=moved, transcendentals=0)


def run_pack(*arrays):
    blocks = pl.pallas_call(
        pack_kernel,
        out_shape=jax.ShapeDtypeStruct((32, 8, 16, 128), BF16),
        in_specs=[ANY] * 4,
        out_specs=ANY,
        scratch_shapes=[
            pltpu.VMEM((4, 16, 8192), BF16),
            pltpu.VMEM((32, 8, 16, 128), BF16),
            pltpu.SemaphoreType.DMA((4, PARTS)),
            pltpu.SemaphoreType.DMA((PARTS,)),
        ],
        name="pack",
    )(*arrays)
    return blocks.reshape(256, 16, 128)


def run_unpack(here, blocks, sums):
    return pl.pallas_call(
        unpack_kernel,
        out_shape=[jax.ShapeDtypeStruct((16, 8192), BF16)] * 4
        + [
            jax.ShapeDtypeStruct((3, 3, 1024), F32),
            jax.ShapeDtypeStruct((1, 1024), F32),
        ],
        in_specs=[SM, VM, VM],
        out_specs=[ANY] * 6,
        scratch_shapes=[
            pltpu.VMEM((4, 16, 8192), BF16),
            pltpu.VMEM((3, 3, 1024), F32),
            pltpu.VMEM((1, 1024), F32),
            pltpu.SemaphoreType.DMA((4, PARTS)),
            pltpu.SemaphoreType.DMA((2,)),
        ],
        compiler_params=pltpu.CompilerParams(vmem_limit_bytes=24 << 20),
        name="unpack",
    )(here, blocks.reshape(32, 8, 16, 128), sums)


def run_prep(lens, here, taps, residues, poles, gain):
    shapes = [((PLAN_ROWS, PIECE), F32), ((MAT_ROWS, 256), BF16)]
    return pl.pallas_call(
        prep_kernel,
        out_shape=[jax.ShapeDtypeStruct(*shape) for shape in shapes],
        in_specs=[SM, SM, VM, VM, VM, VM],
        out_specs=[VM] * 2,
        scratch_shapes=[pltpu.VMEM((PIECE, PIECE), F32)],
        cost_estimate=cost(4_000_000, 1 << 20),
        name="prep",
    )(lens, here, taps, residues, poles, gain)


def run_main(meta, blocks, plan, mats):
    scratch = [
        pltpu.SMEM((NPIECES + 1,), jnp.int32),
        pltpu.VMEM((NPIECES + 1, PIECE, PIECE), F32),
        pltpu.VMEM((NPIECES, 96, PIECE), F32),
        pltpu.VMEM((NPIECES, OWN, PIECE), F32),
        pltpu.VMEM((NPIECES, OWN, PIECE), F32),
        pltpu.VMEM((2, VROWS, 256), BF16),
        pltpu.VMEM((2, VROWS, 256), BF16),
        pltpu.VMEM((VROWS, 256), F32),
        pltpu.VMEM((VROWS, 256), F32),
        pltpu.VMEM((VROWS, PIECE), F32),
        pltpu.VMEM((VROWS, PIECE), F32),
        pltpu.VMEM((NPIECES + 1, 96, PIECE), F32),
        pltpu.VMEM((NPIECES, PIECE, PIECE), BF16),
        pltpu.VMEM((256, 16, 128), BF16),
        pltpu.VMEM((3, PIECE, PIECE), F32),
        pltpu.SemaphoreType.DMA((4,)),
    ]
    return pl.pallas_call(
        main_kernel,
        out_shape=[
            jax.ShapeDtypeStruct((256, 16, 128), BF16),
            jax.ShapeDtypeStruct((4, 128), F32),
        ],
        in_specs=[SM, VM, VM, VM],
        out_specs=[ANY, VM],
        scratch_shapes=scratch,
        compiler_params=pltpu.CompilerParams(vmem_limit_bytes=LIMIT_MB << 20),
        name="block",
    )(meta, blocks, plan, mats)


def exchange(blocks):
    return lax.all_to_all(blocks, BOTH, split_axis=0, concat_axis=0, tiled=True)


def gather_sums(sums):
    held = sums[None]
    for flips in ((8, 16, 24), (1, 2, 3), (4,)):
        got = [held]
        for flip in flips:
            pairs = [(i, i ^ flip) for i in range(32)]
            got.append(lax.ppermute(held, "ctx", pairs))
        held = jnp.concatenate(got, axis=0)
    return held


def local(
    gate_rows,
    key_rows,
    value_rows,
    out_grad,
    conv_taps,
    filter_residues,
    filter_poles,
    skip_gain,
    seq_lengths,
    piece_list,
):
    here = lax.axis_index("ctx").astype(jnp.int32).reshape(1)
    blocks = exchange(run_pack(gate_rows, key_rows, value_rows, out_grad))
    plan, mats = run_prep(
        seq_lengths,
        here,
        conv_taps,
        filter_residues,
        filter_poles,
        skip_gain.reshape(1, -1),
    )
    plan = jnp.pad(plan, ((0, 8), (0, 0)))
    mats = jnp.pad(mats, ((0, 16), (0, 0)))
    meta = jnp.concatenate([seq_lengths, piece_list, here])
    results, sums = run_main(meta, blocks, plan, mats)
    *outs, taps_grad, skip_grad = run_unpack(here, exchange(results), gather_sums(sums))
    return (*outs, taps_grad, skip_grad.reshape(1024))


def solution(mesh):
    rows = P(BOTH, None)
    return jax.shard_map(
        local,
        mesh=mesh,
        in_specs=(
            rows, rows, rows, rows,
            P(None, None, "mp"), P("mp", None), P("mp", None), P("mp"), P(), P(),
        ),
        out_specs=(rows, rows, rows, rows, P(None, None, "mp"), P("mp")),
        check_vma=False,
    )
```

```python
import math

import jax
import jax.numpy as jnp
from jax import lax
from jax.experimental import pallas as pl
from jax.experimental.pallas import tpu as pltpu
from jax.sharding import PartitionSpec as P

BOTH = ("ctx", "mp")
PIECE = 128
NPIECES = 32
NSEQ = 8
MODES = 16
OWN = 32
TOKENS = 4096
BASE = NPIECES * 16
VROWS = BASE + NSEQ * 16
PARTS = 4
PART = 8192 // PARTS
CHUNK = 4
MASKS = 9 * NPIECES
PLAN_ROWS = MASKS + 3 * 96 + OWN
T_AHEAD, T_BACK, C_AHEAD, C_BACK, E_BOTH = 0, 512, 1024, 1152, 1280
MAT_ROWS = 1792
LIMIT_MB = 48
F32 = jnp.float32
BF16 = jnp.bfloat16


def lane_ids(shape):
    return lax.broadcasted_iota(jnp.int32, shape, 1)


def block_ids():
    return lane_ids((16, PIECE)) // OWN


def pack_kernel(a_ref, b_ref, c_ref, d_ref, out_ref, stage_ref, o_ref, sem, out_sem):
    refs = (a_ref, b_ref, c_ref, d_ref)

    def copy(a, part):
        cols = pl.ds(part * PART, PART)
        return pltpu.make_async_copy(
            refs[a].at[:, cols], stage_ref.at[a, :, cols], sem.at[a, part]
        )

    def send(part):
        js = pl.ds(part * (8 // PARTS), 8 // PARTS)
        return pltpu.make_async_copy(o_ref.at[:, js], out_ref.at[:, js], out_sem.at[part])

    for part in range(PARTS):
        for a in range(4):
            copy(a, part).start()
    spot = block_ids()
    for part in range(PARTS):
        for a in range(4):
            copy(a, part).wait()

        def step(i, carry):
            at = part * (64 // PARTS) + i
            cols = pl.ds(pl.multiple_of(at * PIECE, PIECE), PIECE)
            turned = [
                pltpu.roll(stage_ref[a, :, cols].astype(F32), OWN * a, 1) if a
                else stage_ref[a, :, cols].astype(F32)
                for a in range(4)
            ]
            for k in range(4):
                tile = turned[(3 - k) % 4]
                for pos in range(3):
                    tile = jnp.where(spot == pos, turned[(pos - k) % 4], tile)
                o_ref[4 * (at % 8) + k, at // 8] = tile.astype(BF16)
            return carry

        lax.fori_loop(0, 64 // PARTS, step, 0, unroll=64 // PARTS)
        send(part).start()
    for part in range(PARTS):
        send(part).wait()


def place_sums(here, parts_ref, taps_ref, skip_ref):
    spot = lane_ids((8, PIECE)) // OWN

    def order(flip):
        return (flip >> 3) + 4 * (flip & 3) + 16 * ((flip >> 2) & 1)

    for j in range(3):
        rows = []
        for k in range(4):
            picked = [
                parts_ref[order((4 * q + k) ^ here), j : j + 1, :] for q in range(8)
            ]
            rows.append(jnp.concatenate(picked, axis=0))
        for a in range(4 if j == 0 else 3):
            moved = [
                pltpu.roll(rows[k], ((k - a) % 4) * OWN, 1) if k != a else rows[k]
                for k in range(4)
            ]
            line = moved[3]
            for k in range(3):
                line = jnp.where(spot == k, moved[k], line)
            for q in range(8):
                cols = slice(q * PIECE, (q + 1) * PIECE)
                if a < 3:
                    taps_ref[a, j : j + 1, cols] = line[q : q + 1]
                else:
                    skip_ref[0:1, cols] = line[q : q + 1]


def unpack_kernel(
    here_ref, x_ref, parts_ref, a_ref, b_ref, c_ref, d_ref, taps_ref, skip_ref,
    stage_ref, tapv_ref, skipv_ref, sem, small_sem,
):
    refs = (a_ref, b_ref, c_ref, d_ref)

    def copy(a, part):
        cols = pl.ds(part * PART, PART)
        return pltpu.make_async_copy(
            stage_ref.at[a, :, cols], refs[a].at[:, cols], sem.at[a, part]
        )

    spot = block_ids()
    for part in range(PARTS):

        def step(i, carry):
            at = part * (64 // PARTS) + i
            cols = pl.ds(pl.multiple_of(at * PIECE, PIECE), PIECE)
            tiles = [x_ref[4 * (at % 8) + k, at // 8].astype(F32) for k in range(4)]
            for a in range(4):
                mixed = tiles[(3 - a) % 4]
                for pos in range(3):
                    mixed = jnp.where(spot == pos, tiles[(pos - a) % 4], mixed)
                if a:
                    mixed = pltpu.roll(mixed, PIECE - OWN * a, 1)
                stage_ref[a, :, cols] = mixed.astype(BF16)
            return carry

        lax.fori_loop(0, 64 // PARTS, step, 0, unroll=64 // PARTS)
        for a in range(4):
            copy(a, part).start()
    place_sums(here_ref[0], parts_ref, tapv_ref, skipv_ref)
    taps_out = pltpu.make_async_copy(tapv_ref, taps_ref, small_sem.at[0])
    skip_out = pltpu.make_async_copy(skipv_ref, skip_ref, small_sem.at[1])
    taps_out.start()
    skip_out.start()
    for part in range(PARTS):
        for a in range(4):
            copy(a, part).wait()
    taps_out.wait()
    skip_out.wait()


def split(values):
    high = values.astype(BF16)
    return high, (values - high.astype(F32)).astype(BF16)


def dot3(left, right):
    left = jnp.concatenate([left[0], left[1], left[0]], axis=1)
    right = jnp.concatenate([right[0], right[0], right[1]], axis=0)
    return jnp.dot(left, right, preferred_element_type=F32)


(M_ONE, M_TWO, L_ONE, L_TWO, FIRST, TAIL, NOTBEG, NEXTCONT, WHOLE) = range(9)


def begins_of(lens_ref):
    begins = [jnp.int32(0)]
    for k in range(NSEQ):
        begins.append(begins[-1] + lens_ref[k])
    return begins


def prep_kernel(
    lens_ref, here_ref, taps_ref, res_ref, pole_ref, gain_ref,
    plan_ref, mats_ref,
    prep_ref,
):
    mask_ref = plan_ref.at[0:MASKS]
    tapb_ref = plan_ref.at[MASKS:]
    here = here_ref[0]
    begins = begins_of(lens_ref)

    shape = (NPIECES, PIECE)
    base = lax.broadcasted_iota(jnp.int32, shape, 0) * PIECE
    row = base + lane_ids(shape)

    def count(ids, upto=NSEQ):
        total = jnp.zeros(shape, jnp.int32)
        for k in range(upto):
            total = total + (begins[k] <= ids).astype(jnp.int32)
        return total

    def starts(ids):
        hit = ids == begins[0]
        for k in range(1, NSEQ + 1):
            hit = hit | (ids == begins[k])
        return hit

    own = count(row)
    at_first, at_last, before = count(base), count(base + PIECE - 1), count(base - 1)
    here_start, prior_start = starts(row), starts(row - 1)
    next_start, after_start = starts(row + 1), starts(row + 2)
    one = jnp.ones(shape, F32)
    zero = jnp.zeros(shape, F32)
    mask_ref[0:32, :] = jnp.where(here_start, zero, one)
    mask_ref[32:64, :] = jnp.where(here_start | prior_start, zero, one)
    mask_ref[64:96, :] = jnp.where(next_start, zero, one)
    mask_ref[96:128, :] = jnp.where(next_start | after_start, zero, one)
    mask_ref[128:160, :] = jnp.where(own == at_first, one, zero)
    mask_ref[160:192, :] = jnp.where(own == at_last, one, zero)
    mask_ref[192:224, :] = jnp.where(at_first == before, one, zero)
    mask_ref[224:256, :] = jnp.where(starts(base + PIECE), zero, one)

    block = pl.ds(pl.multiple_of((here // 4) * 128, 128), 128)
    shift = lax.rem(128 - 32 * lax.rem(here, 4), 128)
    prep_ref[...] = jnp.zeros((PIECE, PIECE), F32)
    for a in range(3):
        for j in range(3):
            prep_ref[a * 3 + j : a * 3 + j + 1, :] = taps_ref[a, j : j + 1, block]
    prep_ref[9:10, :] = gain_ref[0:1, block]
    prep_ref[0:16, :] = pltpu.roll(prep_ref[0:16, :], shift, 1)
    prep_ref[16:18, 0:MODES] = pole_ref[pl.ds(2 * here, 2), :]
    prep_ref[24:26, 0:MODES] = res_ref[pl.ds(2 * here, 2), :]
    turned = prep_ref[...].T

    def column(rows, at):
        return jnp.broadcast_to(turned[0:rows, at : at + 1], (rows, PIECE))

    for j in range(3):
        for a in range(3):
            tapb_ref[j * 96 + a * OWN : j * 96 + (a + 1) * OWN, :] = column(OWN, a * 3 + j)
    tapb_ref[288 : 288 + OWN, :] = column(OWN, 9)
    pole = jnp.concatenate([column(MODES, 16), column(MODES, 17)], axis=0)
    residue = jnp.concatenate([column(MODES, 24), column(MODES, 25)], axis=0)
    weight = residue * jnp.sqrt(1.0 - pole * pole)
    lane = lane_ids((2 * MODES, PIECE))
    powers = jnp.ones((2 * MODES, PIECE), F32)
    falling = powers
    square = pole
    for bit in range(7):
        up = ((lane >> bit) & 1) == 1
        powers = jnp.where(up, powers * square, powers)
        falling = jnp.where(up, falling, falling * square)
        square = square * square
    rising = weight * (powers * pole)
    shrinking = weight * (falling * pole)
    taper = weight * powers

    sub_ids = lax.broadcasted_iota(jnp.int32, (PIECE, PIECE), 0)
    col_ids = lane_ids((PIECE, PIECE))
    mats_ref[...] = jnp.zeros(mats_ref.shape, BF16)
    for g in range(2):
        line = jnp.sum(taper[g * MODES : (g + 1) * MODES], axis=0, keepdims=True)
        spread = pltpu.roll(
            jnp.broadcast_to(line, (PIECE, PIECE)), 0, 1, stride=1, stride_axis=0
        )
        toeplitz = jnp.where(col_ids >= sub_ids, spread, 0.0)
        at = slice(g * PIECE, (g + 1) * PIECE)
        for start, square_tile in ((T_AHEAD, toeplitz), (T_BACK, toeplitz.T)):
            for part, tile in enumerate(split(square_tile)):
                top = start + part * 256 + g * PIECE
                mats_ref[top : top + PIECE, at] = tile
        for start, source in ((C_AHEAD, rising), (C_BACK, shrinking)):
            high, low = split(source[g * MODES : (g + 1) * MODES])
            for top, tile in ((0, high), (32, high), (64, low)):
                top = start + top + g * MODES
                mats_ref[top : top + MODES, at] = tile
    blank = jnp.zeros((32, PIECE), F32)
    fall_cols = jnp.concatenate([falling, falling, falling, blank], axis=0).T
    power_cols = jnp.concatenate([powers, powers, powers, blank], axis=0).T
    group_zero = (col_ids & 16) == 0
    for half, cols in enumerate((fall_cols, power_cols)):
        at = slice(half * PIECE, (half + 1) * PIECE)
        for part, tile in enumerate(split(cols)):
            wide = tile.astype(F32)
            top = E_BOTH + part * 256
            mats_ref[top : top + PIECE, at] = jnp.where(group_zero, wide, 0.0).astype(BF16)
            mats_ref[top + PIECE : top + 256, at] = jnp.where(group_zero, 0.0, wide).astype(BF16)
    leap = fall_cols[0:1, :] * fall_cols[126:127, :]
    mask_ref[256:288, :] = leap * jnp.where(at_first == at_last, one, zero)

def store_lhs(ref, at, values):
    for part, tile in enumerate(split(values)):
        ref[part, pl.ds(at, 16), 0:PIECE] = tile[0:16]
        ref[part, pl.ds(at, 16), PIECE:] = tile[16:32]


def unrolled(count, body, carry):
    for i in range(count):
        carry = body(i, carry)
    return carry


def main_kernel(
    meta_ref, x_ref, plan_ref, mats_ref,
    out_ref, g_ref,
    inv_ref, xt_ref, feat_ref, z_ref, gu_ref, lzf_ref, lgt_ref,
    u_ref, gz_ref, e_ref, h_ref, gs_ref, ys_ref, y_ref, acc_ref, sem,
):
    lens_ref = meta_ref
    here = meta_ref[NSEQ + NPIECES]
    turn = lax.rem(here, 4)

    def place(pos):
        return pl.ds(pl.multiple_of(lax.rem(pos + turn, 4) * OWN, OWN), OWN)

    def unplace(pos):
        return pl.ds(pl.multiple_of(lax.rem(pos + 4 - turn, 4) * OWN, OWN), OWN)

    begins = begins_of(lens_ref)

    def invert(s, carry):
        inv_ref[meta_ref[NSEQ + s]] = s
        return carry

    lax.fori_loop(0, NPIECES, invert, 0, unroll=4)
    gs_ref[NPIECES] = jnp.zeros((96, PIECE), F32)
    acc_ref[...] = jnp.zeros(acc_ref.shape, F32)
    blank = jnp.zeros((OWN, PIECE), F32)

    def turn_in(p):
        tile = x_ref[pl.ds(inv_ref[p] * 8, 8)].reshape(PIECE, PIECE)
        tile = tile.T.astype(F32)
        for pos in range(4):
            xt_ref[p, unplace(pos), :] = tile[pos * OWN : (pos + 1) * OWN]

    lane = lane_ids((OWN, PIECE))

    def mask(which, p):
        return plan_ref[pl.ds(which * NPIECES + p, 1), :]

    def part(a):
        return slice(a * OWN, (a + 1) * OWN)

    def tap(j, a):
        top = MASKS + j * 96 + a * OWN
        return plan_ref[top : top + OWN, :]

    def mats(top, depth, cols=slice(0, 256)):
        return mats_ref[top : top + depth, cols], mats_ref[top + depth : top + 2 * depth, cols]

    def ahead(chunk, carry):
        pieces = range(chunk * CHUNK, (chunk + 1) * CHUNK)
        for p in pieces:
            turn_in(p)
        for a in range(3):
            taps = [tap(j, a) for j in range(3)]
            prior = xt_ref[pieces[0] - 1, part(a), :] if chunk else blank
            for p in pieces:
                x = xt_ref[p, part(a), :]
                x_one = pltpu.roll(jnp.where(lane == PIECE - 1, prior, x), 1, 1)
                x_two = pltpu.roll(jnp.where(lane >= PIECE - 2, prior, x), 2, 1)
                feat_ref[p, part(a), :] = (
                    taps[0] * x
                    + mask(M_ONE, p) * (taps[1] * x_one)
                    + mask(M_TWO, p) * (taps[2] * x_two)
                )
                prior = x
        skip = jnp.zeros((OWN, PIECE), F32)
        for p in pieces:
            z = feat_ref[p, part(1), :] * feat_ref[p, part(2), :]
            gu = xt_ref[p, part(3), :] * feat_ref[p, part(0), :]
            z_ref[p] = z
            gu_ref[p] = gu
            skip = skip + gu * z
            store_lhs(lzf_ref, p * 16, z * mask(FIRST, p))
            store_lhs(lgt_ref, p * 16, gu * mask(TAIL, p))
        acc_ref[0, part(3), :] += skip
        return carry

    unrolled(NPIECES // CHUNK, ahead, 0)

    line = lane_ids((1, PIECE))
    extras = []
    for k in range(1, NSEQ):
        p = begins[k] // PIECE
        rows = p * PIECE + line
        inner = lax.rem(begins[k], PIECE) != 0
        later = (rows >= begins[k]) & (rows < begins[k + 1]) & inner
        sooner = (rows >= begins[k - 1]) & (rows < begins[k]) & inner
        later = jnp.where(later, 1.0, 0.0)
        sooner = jnp.where(sooner, 1.0, 0.0)
        extras.append((p, later, sooner, inner))
        store_lhs(lzf_ref, BASE + (k - 1) * 16, z_ref[p] * later)
        store_lhs(lgt_ref, BASE + (k - 1) * 16, gu_ref[p] * sooner)
    none = jnp.zeros((OWN, PIECE), F32)
    store_lhs(lzf_ref, VROWS - 16, none)
    store_lhs(lgt_ref, VROWS - 16, none)

    def both(ref):
        return ref[0], ref[1]

    e_ref[...] = dot3(both(lzf_ref), mats(E_BOTH, 256, slice(0, PIECE)))
    h_ref[...] = dot3(both(lgt_ref), mats(E_BOTH, 256, slice(PIECE, 256)))
    for ref, ks in ((e_ref, range(NSEQ - 1)), (h_ref, range(NSEQ - 2, -1, -1))):
        for k in ks:
            p, _, _, inner = extras[k]
            at = pl.ds(pl.multiple_of(p * 16, 16), 16)
            ref[at, :] = jnp.where(inner, ref[BASE + k * 16 : BASE + (k + 1) * 16, :], ref[at, :])

    def scan(step, carry):
        state, back = carry
        p = step
        at = pl.ds(p * 16, 16)
        found = e_ref[at, :]
        state = state * mask(NOTBEG, p)
        e_ref[at, :] = state
        state = found + mask(WHOLE, p) * state
        p = NPIECES - 1 - step
        at = pl.ds(p * 16, 16)
        found = h_ref[at, :]
        back = back * mask(NEXTCONT, p)
        h_ref[at, :] = back
        back = found + mask(WHOLE, p) * back
        return state, back

    idle = jnp.zeros((16, PIECE), F32)
    unrolled(NPIECES, scan, (idle, idle))

    def three(states):
        high = states.astype(BF16).astype(F32)
        lane = lane_ids(states.shape)
        low = (lane >= 32) & (lane < 64)
        return jnp.where(low, states - high, high).astype(BF16)

    u_ref[...] = dot3(both(lzf_ref), mats(T_AHEAD, 256))
    gz_ref[...] = dot3(both(lgt_ref), mats(T_BACK, 256))
    u_ref[0:BASE, :] += jnp.dot(three(e_ref[0:BASE, :]), mats_ref[C_AHEAD : C_AHEAD + PIECE, :], preferred_element_type=F32)
    gz_ref[0:BASE, :] += jnp.dot(three(h_ref[0:BASE, :]), mats_ref[C_BACK : C_BACK + PIECE, :], preferred_element_type=F32)
    for k, (p, later, sooner, _) in enumerate(extras):
        at = pl.ds(pl.multiple_of(p * 16, 16), 16)
        more = slice(BASE + k * 16, BASE + (k + 1) * 16)
        for ref, kept in ((u_ref, later), (gz_ref, sooner)):
            for half in (slice(0, PIECE), slice(PIECE, 2 * PIECE)):
                ref[at, half] = jnp.where(kept > 0.0, ref[more, half], ref[at, half])

    def gradients(p, carry):
        at = pl.ds(p * 16, 16)
        gain = tap(3, 0)
        u = jnp.concatenate([u_ref[at, 0:PIECE], u_ref[at, PIECE:]], axis=0)
        gz = jnp.concatenate([gz_ref[at, 0:PIECE], gz_ref[at, PIECE:]], axis=0)
        filtered = u + gain * z_ref[p]
        gz = gz + gain * gu_ref[p]
        ys_ref[p, place(0), :] = (feat_ref[p, part(0), :] * filtered).astype(BF16)
        gs_ref[p, part(0), :] = xt_ref[p, part(3), :] * filtered
        gs_ref[p, part(1), :] = gz * feat_ref[p, part(2), :]
        gs_ref[p, part(2), :] = gz * feat_ref[p, part(1), :]
        return carry

    unrolled(NPIECES, gradients, 0)

    def send(p):
        return pltpu.make_async_copy(
            y_ref.at[pl.ds(p * 64, 64)], out_ref.at[pl.ds(p * 64, 64)], sem.at[p]
        )

    def behind(chunk, carry):
        for a in range(3):
            taps = [tap(j, a) for j in range(3)]
            sums = [jnp.zeros((OWN, PIECE), F32) for _ in range(3)]
            after = gs_ref[(chunk + 1) * CHUNK, part(a), :]
            for p in reversed(range(chunk * CHUNK, (chunk + 1) * CHUNK)):
                grad = gs_ref[p, part(a), :]
                x = xt_ref[p, part(a), :]
                g_one = pltpu.roll(jnp.where(lane == 0, after, grad), PIECE - 1, 1)
                g_two = pltpu.roll(jnp.where(lane < 2, after, grad), PIECE - 2, 1)
                g_one = mask(L_ONE, p) * g_one
                g_two = mask(L_TWO, p) * g_two
                back = taps[0] * grad + taps[1] * g_one + taps[2] * g_two
                ys_ref[p, place(a + 1), :] = back.astype(BF16)
                for j, g in enumerate((grad, g_one, g_two)):
                    sums[j] = sums[j] + g * x
                after = grad
            for j in range(3):
                acc_ref[j, part(a), :] += sums[j]
        return carry

    unrolled(NPIECES // CHUNK, behind, 0)
    for part in range(4):
        for s in range(part * 8, part * 8 + 8):
            tile = ys_ref[meta_ref[NSEQ + s]].T
            y_ref[s * 8 : s * 8 + 8] = tile.reshape(8, 16, PIECE)
        send(part).start()

    norm = 1.0 / math.sqrt(TOKENS)
    g_ref[3:4, :] = jnp.zeros((1, PIECE), F32)
    for j in range(3):
        g_ref[j : j + 1, :] = norm * jnp.sum(acc_ref[j].T, axis=0, keepdims=True)
    for p in range(4):
        send(p).wait()


VM = pl.BlockSpec(memory_space=pltpu.VMEM)
SM = pl.BlockSpec(memory_space=pltpu.SMEM)
ANY = pl.BlockSpec(memory_space=pl.ANY)


def cost(flops, moved):
    return pl.CostEstimate(flops=flops, bytes_accessed=moved, transcendentals=0)


def run_pack(*arrays):
    blocks = pl.pallas_call(
        pack_kernel,
        out_shape=jax.ShapeDtypeStruct((32, 8, 16, 128), BF16),
        in_specs=[ANY] * 4,
        out_specs=ANY,
        scratch_shapes=[
            pltpu.VMEM((4, 16, 8192), BF16),
            pltpu.VMEM((32, 8, 16, 128), BF16),
            pltpu.SemaphoreType.DMA((4, PARTS)),
            pltpu.SemaphoreType.DMA((PARTS,)),
        ],
        name="pack",
    )(*arrays)
    return blocks.reshape(256, 16, 128)


def run_unpack(here, blocks, sums):
    return pl.pallas_call(
        unpack_kernel,
        out_shape=[jax.ShapeDtypeStruct((16, 8192), BF16)] * 4
        + [
            jax.ShapeDtypeStruct((3, 3, 1024), F32),
            jax.ShapeDtypeStruct((1, 1024), F32),
        ],
        in_specs=[SM, VM, VM],
        out_specs=[ANY] * 6,
        scratch_shapes=[
            pltpu.VMEM((4, 16, 8192), BF16),
            pltpu.VMEM((3, 3, 1024), F32),
            pltpu.VMEM((1, 1024), F32),
            pltpu.SemaphoreType.DMA((4, PARTS)),
            pltpu.SemaphoreType.DMA((2,)),
        ],
        compiler_params=pltpu.CompilerParams(vmem_limit_bytes=24 << 20),
        name="unpack",
    )(here, blocks.reshape(32, 8, 16, 128), sums)


def run_prep(lens, here, taps, residues, poles, gain):
    shapes = [((PLAN_ROWS, PIECE), F32), ((MAT_ROWS, 256), BF16)]
    return pl.pallas_call(
        prep_kernel,
        out_shape=[jax.ShapeDtypeStruct(*shape) for shape in shapes],
        in_specs=[SM, SM, VM, VM, VM, VM],
        out_specs=[VM] * 2,
        scratch_shapes=[pltpu.VMEM((PIECE, PIECE), F32)],
        cost_estimate=cost(4_000_000, 1 << 20),
        name="prep",
    )(lens, here, taps, residues, poles, gain)


def run_main(meta, blocks, plan, mats):
    scratch = [
        pltpu.SMEM((NPIECES,), jnp.int32),
        pltpu.VMEM((NPIECES, PIECE, PIECE), F32),
        pltpu.VMEM((NPIECES, 96, PIECE), F32),
        pltpu.VMEM((NPIECES, OWN, PIECE), F32),
        pltpu.VMEM((NPIECES, OWN, PIECE), F32),
        pltpu.VMEM((2, VROWS, 256), BF16),
        pltpu.VMEM((2, VROWS, 256), BF16),
        pltpu.VMEM((VROWS, 256), F32),
        pltpu.VMEM((VROWS, 256), F32),
        pltpu.VMEM((VROWS, PIECE), F32),
        pltpu.VMEM((VROWS, PIECE), F32),
        pltpu.VMEM((NPIECES + 1, 96, PIECE), F32),
        pltpu.VMEM((NPIECES, PIECE, PIECE), BF16),
        pltpu.VMEM((256, 16, PIECE), BF16),
        pltpu.VMEM((3, PIECE, PIECE), F32),
        pltpu.SemaphoreType.DMA((4,)),
    ]
    return pl.pallas_call(
        main_kernel,
        out_shape=[
            jax.ShapeDtypeStruct((256, 16, 128), BF16),
            jax.ShapeDtypeStruct((4, 128), F32),
        ],
        in_specs=[SM, VM, VM, VM],
        out_specs=[ANY, VM],
        scratch_shapes=scratch,
        compiler_params=pltpu.CompilerParams(vmem_limit_bytes=LIMIT_MB << 20),
        name="block",
    )(meta, blocks, plan, mats)


def exchange(blocks):
    return lax.all_to_all(blocks, BOTH, split_axis=0, concat_axis=0, tiled=True)


def gather_sums(sums):
    held = sums[None]
    for flips in ((8, 16, 24), (1, 2, 3), (4,)):
        got = [held]
        for flip in flips:
            pairs = [(i, i ^ flip) for i in range(32)]
            got.append(lax.ppermute(held, "ctx", pairs))
        held = jnp.concatenate(got, axis=0)
    return held


def local(
    gate_rows,
    key_rows,
    value_rows,
    out_grad,
    conv_taps,
    filter_residues,
    filter_poles,
    skip_gain,
    seq_lengths,
    piece_list,
):
    here = lax.axis_index("ctx").astype(jnp.int32).reshape(1)
    blocks = exchange(run_pack(gate_rows, key_rows, value_rows, out_grad))
    plan, mats = run_prep(
        seq_lengths,
        here,
        conv_taps,
        filter_residues,
        filter_poles,
        skip_gain.reshape(1, -1),
    )
    plan = jnp.pad(plan, ((0, 8), (0, 0)))
    mats = jnp.pad(mats, ((0, 16), (0, 0)))
    meta = jnp.concatenate([seq_lengths, piece_list, here])
    results, sums = run_main(meta, blocks, plan, mats)
    *outs, taps_grad, skip_grad = run_unpack(here, exchange(results), gather_sums(sums))
    return (*outs, taps_grad, skip_grad.reshape(1024))


def solution(mesh):
    rows = P(BOTH, None)
    return jax.shard_map(
        local,
        mesh=mesh,
        in_specs=(
            rows, rows, rows, rows,
            P(None, None, "mp"), P("mp", None), P("mp", None), P("mp"), P(), P(),
        ),
        out_specs=(rows, rows, rows, rows, P(None, None, "mp"), P("mp")),
        check_vma=False,
    )
```

```python
import math

import jax
import jax.numpy as jnp
from jax import lax
from jax.experimental import pallas as pl
from jax.experimental.pallas import tpu as pltpu
from jax.sharding import PartitionSpec as P

BOTH = ("ctx", "mp")
PIECE = 128
NPIECES = 32
NSEQ = 8
MODES = 16
OWN = 32
TOKENS = 4096
BASE = NPIECES * 16
VROWS = BASE + NSEQ * 16
PARTS = 4
PART = 8192 // PARTS
CHUNK = 4
MASKS = 9 * NPIECES
PLAN_ROWS = MASKS + 3 * 96 + OWN
T_AHEAD, T_BACK, C_AHEAD, C_BACK, E_BOTH = 0, 512, 1024, 1152, 1280
MAT_ROWS = 1792
LIMIT_MB = 48
F32 = jnp.float32
BF16 = jnp.bfloat16


def lane_ids(shape):
    return lax.broadcasted_iota(jnp.int32, shape, 1)


def block_ids():
    return lane_ids((16, PIECE)) // OWN


def pack_kernel(a_ref, b_ref, c_ref, d_ref, out_ref, stage_ref, o_ref, sem, out_sem):
    refs = (a_ref, b_ref, c_ref, d_ref)

    def copy(a, part):
        cols = pl.ds(part * PART, PART)
        return pltpu.make_async_copy(
            refs[a].at[:, cols], stage_ref.at[a, :, cols], sem.at[a, part]
        )

    def send(part):
        js = pl.ds(part * (8 // PARTS), 8 // PARTS)
        return pltpu.make_async_copy(o_ref.at[:, js], out_ref.at[:, js], out_sem.at[part])

    for part in range(PARTS):
        for a in range(4):
            copy(a, part).start()
    spot = block_ids()
    for part in range(PARTS):
        for a in range(4):
            copy(a, part).wait()

        def step(i, carry):
            at = part * (64 // PARTS) + i
            cols = pl.ds(pl.multiple_of(at * PIECE, PIECE), PIECE)
            turned = [
                pltpu.roll(stage_ref[a, :, cols].astype(F32), OWN * a, 1) if a
                else stage_ref[a, :, cols].astype(F32)
                for a in range(4)
            ]
            for k in range(4):
                tile = turned[(3 - k) % 4]
                for pos in range(3):
                    tile = jnp.where(spot == pos, turned[(pos - k) % 4], tile)
                o_ref[4 * (at % 8) + k, at // 8] = tile.astype(BF16)
            return carry

        lax.fori_loop(0, 64 // PARTS, step, 0, unroll=64 // PARTS)
        send(part).start()
    for part in range(PARTS):
        send(part).wait()


def place_sums(here, parts_ref, taps_ref, skip_ref):
    spot = lane_ids((8, PIECE)) // OWN

    def order(flip):
        return (flip >> 3) + 4 * (flip & 3) + 16 * ((flip >> 2) & 1)

    for j in range(3):
        rows = []
        for k in range(4):
            picked = [
                parts_ref[order((4 * q + k) ^ here), j : j + 1, :] for q in range(8)
            ]
            rows.append(jnp.concatenate(picked, axis=0))
        for a in range(4 if j == 0 else 3):
            moved = [
                pltpu.roll(rows[k], ((k - a) % 4) * OWN, 1) if k != a else rows[k]
                for k in range(4)
            ]
            line = moved[3]
            for k in range(3):
                line = jnp.where(spot == k, moved[k], line)
            for q in range(8):
                cols = slice(q * PIECE, (q + 1) * PIECE)
                if a < 3:
                    taps_ref[a, j : j + 1, cols] = line[q : q + 1]
                else:
                    skip_ref[0:1, cols] = line[q : q + 1]


def unpack_kernel(
    here_ref, x_ref, parts_ref, a_ref, b_ref, c_ref, d_ref, taps_ref, skip_ref,
    stage_ref, tapv_ref, skipv_ref, sem, small_sem,
):
    refs = (a_ref, b_ref, c_ref, d_ref)

    def copy(a, part):
        cols = pl.ds(part * PART, PART)
        return pltpu.make_async_copy(
            stage_ref.at[a, :, cols], refs[a].at[:, cols], sem.at[a, part]
        )

    spot = block_ids()
    for part in range(PARTS):

        def step(i, carry):
            at = part * (64 // PARTS) + i
            cols = pl.ds(pl.multiple_of(at * PIECE, PIECE), PIECE)
            tiles = [x_ref[4 * (at % 8) + k, at // 8].astype(F32) for k in range(4)]
            for a in range(4):
                mixed = tiles[(3 - a) % 4]
                for pos in range(3):
                    mixed = jnp.where(spot == pos, tiles[(pos - a) % 4], mixed)
                if a:
                    mixed = pltpu.roll(mixed, PIECE - OWN * a, 1)
                stage_ref[a, :, cols] = mixed.astype(BF16)
            return carry

        lax.fori_loop(0, 64 // PARTS, step, 0, unroll=64 // PARTS)
        for a in range(4):
            copy(a, part).start()
    place_sums(here_ref[0], parts_ref, tapv_ref, skipv_ref)
    taps_out = pltpu.make_async_copy(tapv_ref, taps_ref, small_sem.at[0])
    skip_out = pltpu.make_async_copy(skipv_ref, skip_ref, small_sem.at[1])
    taps_out.start()
    skip_out.start()
    for part in range(PARTS):
        for a in range(4):
            copy(a, part).wait()
    taps_out.wait()
    skip_out.wait()


def split(values):
    high = values.astype(BF16)
    return high, (values - high.astype(F32)).astype(BF16)


def dot3(left, right):
    left = jnp.concatenate([left[0], left[1], left[0]], axis=1)
    right = jnp.concatenate([right[0], right[0], right[1]], axis=0)
    return jnp.dot(left, right, preferred_element_type=F32)


(M_ONE, M_TWO, L_ONE, L_TWO, FIRST, TAIL, NOTBEG, NEXTCONT, WHOLE) = range(9)


def begins_of(lens_ref):
    begins = [jnp.int32(0)]
    for k in range(NSEQ):
        begins.append(begins[-1] + lens_ref[k])
    return begins


def prep_kernel(
    lens_ref, here_ref, taps_ref, res_ref, pole_ref, gain_ref,
    plan_ref, mats_ref,
    prep_ref,
):
    mask_ref = plan_ref.at[0:MASKS]
    tapb_ref = plan_ref.at[MASKS:]
    here = here_ref[0]
    begins = begins_of(lens_ref)

    shape = (NPIECES, PIECE)
    base = lax.broadcasted_iota(jnp.int32, shape, 0) * PIECE
    row = base + lane_ids(shape)

    def count(ids, upto=NSEQ):
        total = jnp.zeros(shape, jnp.int32)
        for k in range(upto):
            total = total + (begins[k] <= ids).astype(jnp.int32)
        return total

    def starts(ids):
        hit = ids == begins[0]
        for k in range(1, NSEQ + 1):
            hit = hit | (ids == begins[k])
        return hit

    own = count(row)
    at_first, at_last, before = count(base), count(base + PIECE - 1), count(base - 1)
    here_start, prior_start = starts(row), starts(row - 1)
    next_start, after_start = starts(row + 1), starts(row + 2)
    one = jnp.ones(shape, F32)
    zero = jnp.zeros(shape, F32)
    mask_ref[0:32, :] = jnp.where(here_start, zero, one)
    mask_ref[32:64, :] = jnp.where(here_start | prior_start, zero, one)
    mask_ref[64:96, :] = jnp.where(next_start, zero, one)
    mask_ref[96:128, :] = jnp.where(next_start | after_start, zero, one)
    mask_ref[128:160, :] = jnp.where(own == at_first, one, zero)
    mask_ref[160:192, :] = jnp.where(own == at_last, one, zero)
    mask_ref[192:224, :] = jnp.where(at_first == before, one, zero)
    mask_ref[224:256, :] = jnp.where(starts(base + PIECE), zero, one)

    block = pl.ds(pl.multiple_of((here // 4) * 128, 128), 128)
    shift = lax.rem(128 - 32 * lax.rem(here, 4), 128)
    prep_ref[...] = jnp.zeros((PIECE, PIECE), F32)
    for a in range(3):
        for j in range(3):
            prep_ref[a * 3 + j : a * 3 + j + 1, :] = taps_ref[a, j : j + 1, block]
    prep_ref[9:10, :] = gain_ref[0:1, block]
    prep_ref[0:16, :] = pltpu.roll(prep_ref[0:16, :], shift, 1)
    prep_ref[16:18, 0:MODES] = pole_ref[pl.ds(2 * here, 2), :]
    prep_ref[24:26, 0:MODES] = res_ref[pl.ds(2 * here, 2), :]
    turned = prep_ref[...].T

    def column(rows, at):
        return jnp.broadcast_to(turned[0:rows, at : at + 1], (rows, PIECE))

    for j in range(3):
        for a in range(3):
            tapb_ref[j * 96 + a * OWN : j * 96 + (a + 1) * OWN, :] = column(OWN, a * 3 + j)
    tapb_ref[288 : 288 + OWN, :] = column(OWN, 9)
    pole = jnp.concatenate([column(MODES, 16), column(MODES, 17)], axis=0)
    residue = jnp.concatenate([column(MODES, 24), column(MODES, 25)], axis=0)
    weight = residue * jnp.sqrt(1.0 - pole * pole)
    lane = lane_ids((2 * MODES, PIECE))
    powers = jnp.ones((2 * MODES, PIECE), F32)
    falling = powers
    square = pole
    for bit in range(7):
        up = ((lane >> bit) & 1) == 1
        powers = jnp.where(up, powers * square, powers)
        falling = jnp.where(up, falling, falling * square)
        square = square * square
    rising = weight * (powers * pole)
    shrinking = weight * (falling * pole)
    taper = weight * powers

    sub_ids = lax.broadcasted_iota(jnp.int32, (PIECE, PIECE), 0)
    col_ids = lane_ids((PIECE, PIECE))
    mats_ref[...] = jnp.zeros(mats_ref.shape, BF16)
    for g in range(2):
        line = jnp.sum(taper[g * MODES : (g + 1) * MODES], axis=0, keepdims=True)
        spread = pltpu.roll(
            jnp.broadcast_to(line, (PIECE, PIECE)), 0, 1, stride=1, stride_axis=0
        )
        toeplitz = jnp.where(col_ids >= sub_ids, spread, 0.0)
        at = slice(g * PIECE, (g + 1) * PIECE)
        for start, square_tile in ((T_AHEAD, toeplitz), (T_BACK, toeplitz.T)):
            for part, tile in enumerate(split(square_tile)):
                top = start + part * 256 + g * PIECE
                mats_ref[top : top + PIECE, at] = tile
        for start, source in ((C_AHEAD, rising), (C_BACK, shrinking)):
            high, low = split(source[g * MODES : (g + 1) * MODES])
            for top, tile in ((0, high), (32, high), (64, low)):
                top = start + top + g * MODES
                mats_ref[top : top + MODES, at] = tile
    blank = jnp.zeros((32, PIECE), F32)
    fall_cols = jnp.concatenate([falling, falling, falling, blank], axis=0).T
    power_cols = jnp.concatenate([powers, powers, powers, blank], axis=0).T
    group_zero = (col_ids & 16) == 0
    for half, cols in enumerate((fall_cols, power_cols)):
        at = slice(half * PIECE, (half + 1) * PIECE)
        for part, tile in enumerate(split(cols)):
            wide = tile.astype(F32)
            top = E_BOTH + part * 256
            mats_ref[top : top + PIECE, at] = jnp.where(group_zero, wide, 0.0).astype(BF16)
            mats_ref[top + PIECE : top + 256, at] = jnp.where(group_zero, 0.0, wide).astype(BF16)
    leap = fall_cols[0:1, :] * fall_cols[126:127, :]
    mask_ref[256:288, :] = leap * jnp.where(at_first == at_last, one, zero)

def store_lhs(ref, at, values):
    for part, tile in enumerate(split(values)):
        ref[part, pl.ds(at, 16), 0:PIECE] = tile[0:16]
        ref[part, pl.ds(at, 16), PIECE:] = tile[16:32]


def unrolled(count, body, carry):
    for i in range(count):
        carry = body(i, carry)
    return carry


def main_kernel(
    meta_ref, x_ref, plan_ref, mats_ref,
    out_ref, g_ref,
    inv_ref, xt_ref, feat_ref, z_ref, gu_ref, lzf_ref, lgt_ref,
    u_ref, gz_ref, e_ref, h_ref, gs_ref, ys_ref, y_ref, acc_ref, sem,
):
    lens_ref = meta_ref
    here = meta_ref[NSEQ + NPIECES]
    turn = lax.rem(here, 4)

    def place(pos):
        return pl.ds(pl.multiple_of(lax.rem(pos + turn, 4) * OWN, OWN), OWN)

    def unplace(pos):
        return pl.ds(pl.multiple_of(lax.rem(pos + 4 - turn, 4) * OWN, OWN), OWN)

    begins = begins_of(lens_ref)

    def invert(s, carry):
        inv_ref[meta_ref[NSEQ + s]] = s
        return carry

    lax.fori_loop(0, NPIECES, invert, 0, unroll=4)
    gs_ref[NPIECES] = jnp.zeros((96, PIECE), F32)
    acc_ref[...] = jnp.zeros(acc_ref.shape, F32)
    blank = jnp.zeros((OWN, PIECE), F32)

    def turn_in(p):
        tile = x_ref[pl.ds(inv_ref[p] * 8, 8)].reshape(PIECE, PIECE)
        tile = tile.T.astype(F32)
        for pos in range(4):
            xt_ref[p, unplace(pos), :] = tile[pos * OWN : (pos + 1) * OWN]

    lane = lane_ids((OWN, PIECE))

    def mask(which, p):
        return plan_ref[pl.ds(which * NPIECES + p, 1), :]

    def part(a):
        return slice(a * OWN, (a + 1) * OWN)

    def tap(j, a):
        top = MASKS + j * 96 + a * OWN
        return plan_ref[top : top + OWN, :]

    def mats(top, depth, cols=slice(0, 256)):
        return mats_ref[top : top + depth, cols], mats_ref[top + depth : top + 2 * depth, cols]

    def products(rows):
        z_part = lzf_ref[0, rows, :], lzf_ref[1, rows, :]
        g_part = lgt_ref[0, rows, :], lgt_ref[1, rows, :]
        e_ref[rows, :] = dot3(z_part, mats(E_BOTH, 256, slice(0, PIECE)))
        h_ref[rows, :] = dot3(g_part, mats(E_BOTH, 256, slice(PIECE, 256)))
        u_ref[rows, :] = dot3(z_part, mats(T_AHEAD, 256))
        gz_ref[rows, :] = dot3(g_part, mats(T_BACK, 256))

    def ahead(chunk, carry):
        pieces = range(chunk * CHUNK, (chunk + 1) * CHUNK)
        for p in pieces:
            turn_in(p)
        for a in range(3):
            taps = [tap(j, a) for j in range(3)]
            prior = xt_ref[pieces[0] - 1, part(a), :] if chunk else blank
            for p in pieces:
                x = xt_ref[p, part(a), :]
                x_one = pltpu.roll(jnp.where(lane == PIECE - 1, prior, x), 1, 1)
                x_two = pltpu.roll(jnp.where(lane >= PIECE - 2, prior, x), 2, 1)
                feat_ref[p, part(a), :] = (
                    taps[0] * x
                    + mask(M_ONE, p) * (taps[1] * x_one)
                    + mask(M_TWO, p) * (taps[2] * x_two)
                )
                prior = x
        skip = jnp.zeros((OWN, PIECE), F32)
        for p in pieces:
            z = feat_ref[p, part(1), :] * feat_ref[p, part(2), :]
            gu = xt_ref[p, part(3), :] * feat_ref[p, part(0), :]
            z_ref[p] = z
            gu_ref[p] = gu
            skip = skip + gu * z
            store_lhs(lzf_ref, p * 16, z * mask(FIRST, p))
            store_lhs(lgt_ref, p * 16, gu * mask(TAIL, p))
        acc_ref[0, part(3), :] += skip
        if chunk * CHUNK % 16 == 16 - CHUNK:
            top = (chunk + 1) * CHUNK * 16
            products(slice(top - 256, top))
        return carry

    unrolled(NPIECES // CHUNK, ahead, 0)

    line = lane_ids((1, PIECE))
    extras = []
    for k in range(1, NSEQ):
        p = begins[k] // PIECE
        rows = p * PIECE + line
        inner = lax.rem(begins[k], PIECE) != 0
        later = (rows >= begins[k]) & (rows < begins[k + 1]) & inner
        sooner = (rows >= begins[k - 1]) & (rows < begins[k]) & inner
        later = jnp.where(later, 1.0, 0.0)
        sooner = jnp.where(sooner, 1.0, 0.0)
        extras.append((p, later, sooner, inner))
        store_lhs(lzf_ref, BASE + (k - 1) * 16, z_ref[p] * later)
        store_lhs(lgt_ref, BASE + (k - 1) * 16, gu_ref[p] * sooner)
    none = jnp.zeros((OWN, PIECE), F32)
    store_lhs(lzf_ref, VROWS - 16, none)
    store_lhs(lgt_ref, VROWS - 16, none)

    def both(ref):
        return ref[0], ref[1]

    products(slice(BASE, VROWS))
    for ref, ks in ((e_ref, range(NSEQ - 1)), (h_ref, range(NSEQ - 2, -1, -1))):
        for k in ks:
            p, _, _, inner = extras[k]
            at = pl.ds(pl.multiple_of(p * 16, 16), 16)
            ref[at, :] = jnp.where(inner, ref[BASE + k * 16 : BASE + (k + 1) * 16, :], ref[at, :])

    def scan(step, carry):
        state, back = carry
        p = step
        at = pl.ds(p * 16, 16)
        found = e_ref[at, :]
        state = state * mask(NOTBEG, p)
        e_ref[at, :] = state
        state = found + mask(WHOLE, p) * state
        p = NPIECES - 1 - step
        at = pl.ds(p * 16, 16)
        found = h_ref[at, :]
        back = back * mask(NEXTCONT, p)
        h_ref[at, :] = back
        back = found + mask(WHOLE, p) * back
        return state, back

    idle = jnp.zeros((16, PIECE), F32)
    unrolled(NPIECES, scan, (idle, idle))

    def three(states):
        high = states.astype(BF16).astype(F32)
        lane = lane_ids(states.shape)
        low = (lane >= 32) & (lane < 64)
        return jnp.where(low, states - high, high).astype(BF16)

    u_ref[0:BASE, :] += jnp.dot(three(e_ref[0:BASE, :]), mats_ref[C_AHEAD : C_AHEAD + PIECE, :], preferred_element_type=F32)
    gz_ref[0:BASE, :] += jnp.dot(three(h_ref[0:BASE, :]), mats_ref[C_BACK : C_BACK + PIECE, :], preferred_element_type=F32)
    for k, (p, later, sooner, _) in enumerate(extras):
        at = pl.ds(pl.multiple_of(p * 16, 16), 16)
        more = slice(BASE + k * 16, BASE + (k + 1) * 16)
        for ref, kept in ((u_ref, later), (gz_ref, sooner)):
            for half in (slice(0, PIECE), slice(PIECE, 2 * PIECE)):
                ref[at, half] = jnp.where(kept > 0.0, ref[more, half], ref[at, half])

    def gradients(p, carry):
        at = pl.ds(p * 16, 16)
        gain = tap(3, 0)
        u = jnp.concatenate([u_ref[at, 0:PIECE], u_ref[at, PIECE:]], axis=0)
        gz = jnp.concatenate([gz_ref[at, 0:PIECE], gz_ref[at, PIECE:]], axis=0)
        filtered = u + gain * z_ref[p]
        gz = gz + gain * gu_ref[p]
        ys_ref[p, place(0), :] = (feat_ref[p, part(0), :] * filtered).astype(BF16)
        gs_ref[p, part(0), :] = xt_ref[p, part(3), :] * filtered
        gs_ref[p, part(1), :] = gz * feat_ref[p, part(2), :]
        gs_ref[p, part(2), :] = gz * feat_ref[p, part(1), :]
        return carry

    unrolled(NPIECES, gradients, 0)

    def send(p):
        return pltpu.make_async_copy(
            y_ref.at[pl.ds(p * 64, 64)], out_ref.at[pl.ds(p * 64, 64)], sem.at[p]
        )

    def behind(chunk, carry):
        for a in range(3):
            taps = [tap(j, a) for j in range(3)]
            sums = [jnp.zeros((OWN, PIECE), F32) for _ in range(3)]
            after = gs_ref[(chunk + 1) * CHUNK, part(a), :]
            for p in reversed(range(chunk * CHUNK, (chunk + 1) * CHUNK)):
                grad = gs_ref[p, part(a), :]
                x = xt_ref[p, part(a), :]
                g_one = pltpu.roll(jnp.where(lane == 0, after, grad), PIECE - 1, 1)
                g_two = pltpu.roll(jnp.where(lane < 2, after, grad), PIECE - 2, 1)
                g_one = mask(L_ONE, p) * g_one
                g_two = mask(L_TWO, p) * g_two
                back = taps[0] * grad + taps[1] * g_one + taps[2] * g_two
                ys_ref[p, place(a + 1), :] = back.astype(BF16)
                for j, g in enumerate((grad, g_one, g_two)):
                    sums[j] = sums[j] + g * x
                after = grad
            for j in range(3):
                acc_ref[j, part(a), :] += sums[j]
        return carry

    unrolled(NPIECES // CHUNK, behind, 0)
    for part in range(4):
        for s in range(part * 8, part * 8 + 8):
            tile = ys_ref[meta_ref[NSEQ + s]].T
            y_ref[s * 8 : s * 8 + 8] = tile.reshape(8, 16, PIECE)
        send(part).start()

    norm = 1.0 / math.sqrt(TOKENS)
    g_ref[3:4, :] = jnp.zeros((1, PIECE), F32)
    for j in range(3):
        g_ref[j : j + 1, :] = norm * jnp.sum(acc_ref[j].T, axis=0, keepdims=True)
    for p in range(4):
        send(p).wait()


VM = pl.BlockSpec(memory_space=pltpu.VMEM)
SM = pl.BlockSpec(memory_space=pltpu.SMEM)
ANY = pl.BlockSpec(memory_space=pl.ANY)


def cost(flops, moved):
    return pl.CostEstimate(flops=flops, bytes_accessed=moved, transcendentals=0)


def run_pack(*arrays):
    blocks = pl.pallas_call(
        pack_kernel,
        out_shape=jax.ShapeDtypeStruct((32, 8, 16, 128), BF16),
        in_specs=[ANY] * 4,
        out_specs=ANY,
        scratch_shapes=[
            pltpu.VMEM((4, 16, 8192), BF16),
            pltpu.VMEM((32, 8, 16, 128), BF16),
            pltpu.SemaphoreType.DMA((4, PARTS)),
            pltpu.SemaphoreType.DMA((PARTS,)),
        ],
        name="pack",
    )(*arrays)
    return blocks.reshape(256, 16, 128)


def run_unpack(here, blocks, sums):
    return pl.pallas_call(
        unpack_kernel,
        out_shape=[jax.ShapeDtypeStruct((16, 8192), BF16)] * 4
        + [
            jax.ShapeDtypeStruct((3, 3, 1024), F32),
            jax.ShapeDtypeStruct((1, 1024), F32),
        ],
        in_specs=[SM, VM, VM],
        out_specs=[ANY] * 6,
        scratch_shapes=[
            pltpu.VMEM((4, 16, 8192), BF16),
            pltpu.VMEM((3, 3, 1024), F32),
            pltpu.VMEM((1, 1024), F32),
            pltpu.SemaphoreType.DMA((4, PARTS)),
            pltpu.SemaphoreType.DMA((2,)),
        ],
        compiler_params=pltpu.CompilerParams(vmem_limit_bytes=24 << 20),
        name="unpack",
    )(here, blocks.reshape(32, 8, 16, 128), sums)


def run_prep(lens, here, taps, residues, poles, gain):
    shapes = [((PLAN_ROWS, PIECE), F32), ((MAT_ROWS, 256), BF16)]
    return pl.pallas_call(
        prep_kernel,
        out_shape=[jax.ShapeDtypeStruct(*shape) for shape in shapes],
        in_specs=[SM, SM, VM, VM, VM, VM],
        out_specs=[VM] * 2,
        scratch_shapes=[pltpu.VMEM((PIECE, PIECE), F32)],
        cost_estimate=cost(4_000_000, 1 << 20),
        name="prep",
    )(lens, here, taps, residues, poles, gain)


def run_main(meta, blocks, plan, mats):
    scratch = [
        pltpu.SMEM((NPIECES,), jnp.int32),
        pltpu.VMEM((NPIECES, PIECE, PIECE), F32),
        pltpu.VMEM((NPIECES, 96, PIECE), F32),
        pltpu.VMEM((NPIECES, OWN, PIECE), F32),
        pltpu.VMEM((NPIECES, OWN, PIECE), F32),
        pltpu.VMEM((2, VROWS, 256), BF16),
        pltpu.VMEM((2, VROWS, 256), BF16),
        pltpu.VMEM((VROWS, 256), F32),
        pltpu.VMEM((VROWS, 256), F32),
        pltpu.VMEM((VROWS, PIECE), F32),
        pltpu.VMEM((VROWS, PIECE), F32),
        pltpu.VMEM((NPIECES + 1, 96, PIECE), F32),
        pltpu.VMEM((NPIECES, PIECE, PIECE), BF16),
        pltpu.VMEM((256, 16, PIECE), BF16),
        pltpu.VMEM((3, PIECE, PIECE), F32),
        pltpu.SemaphoreType.DMA((4,)),
    ]
    return pl.pallas_call(
        main_kernel,
        out_shape=[
            jax.ShapeDtypeStruct((256, 16, 128), BF16),
            jax.ShapeDtypeStruct((4, 128), F32),
        ],
        in_specs=[SM, VM, VM, VM],
        out_specs=[ANY, VM],
        scratch_shapes=scratch,
        compiler_params=pltpu.CompilerParams(vmem_limit_bytes=LIMIT_MB << 20),
        name="block",
    )(meta, blocks, plan, mats)


def exchange(blocks):
    return lax.all_to_all(blocks, BOTH, split_axis=0, concat_axis=0, tiled=True)


def gather_sums(sums):
    held = sums[None]
    for flips in ((8, 16, 24), (1, 2, 3), (4,)):
        got = [held]
        for flip in flips:
            pairs = [(i, i ^ flip) for i in range(32)]
            got.append(lax.ppermute(held, "ctx", pairs))
        held = jnp.concatenate(got, axis=0)
    return held


def local(
    gate_rows,
    key_rows,
    value_rows,
    out_grad,
    conv_taps,
    filter_residues,
    filter_poles,
    skip_gain,
    seq_lengths,
    piece_list,
):
    here = lax.axis_index("ctx").astype(jnp.int32).reshape(1)
    blocks = exchange(run_pack(gate_rows, key_rows, value_rows, out_grad))
    plan, mats = run_prep(
        seq_lengths,
        here,
        conv_taps,
        filter_residues,
        filter_poles,
        skip_gain.reshape(1, -1),
    )
    plan = jnp.pad(plan, ((0, 8), (0, 0)))
    mats = jnp.pad(mats, ((0, 16), (0, 0)))
    meta = jnp.concatenate([seq_lengths, piece_list, here])
    results, sums = run_main(meta, blocks, plan, mats)
    *outs, taps_grad, skip_grad = run_unpack(here, exchange(results), gather_sums(sums))
    return (*outs, taps_grad, skip_grad.reshape(1024))


def solution(mesh):
    rows = P(BOTH, None)
    return jax.shard_map(
        local,
        mesh=mesh,
        in_specs=(
            rows, rows, rows, rows,
            P(None, None, "mp"), P("mp", None), P("mp", None), P("mp"), P(), P(),
        ),
        out_specs=(rows, rows, rows, rows, P(None, None, "mp"), P("mp")),
        check_vma=False,
    )
```
